256 devices in a mesh: rows: 64 (over z, y, core), sub: 4 (over x).
Axes of the slice: x: 4, y: 4, z: 8, core: 2. Of those that a mesh axis runs over, the one named last changes fastest.
Arguments:
- embeddings: bfloat16 [131072, 768], P(('rows', 'sub')), may hold values from -0.25 to 0.25
- factor: float32 [131072, 512], P(('rows', 'sub')), may hold values from -0.15 to 0.15
- diagonal: float32 [131072], P(('rows', 'sub')), may hold values from 0.5 to 1
- pivot_owner: int32 [4, 256], replicated, may hold values from 0 to 255, as said below
- pivot_local: int32 [4, 256], replicated, may hold values from 0 to 511, as said below
Outputs:
- new_columns: float32 [131072, 1024], P(('rows', 'sub'))
- new_diagonal: float32 [131072], P(('rows', 'sub'))
The draws below stay inside these ranges and needn't reach their ends.
Inputs may be any that keep to these rules, and one draw needn't show every extreme that they name: The 1024 global rows pivot_owner * 512 + pivot_local are all different; row 0 and the last row of all are among them. `pivot_local`: read together with pivot_owner.
All inputs are finite; a program needn't handle non-finite values.
Results may differ from the reference program's by a relative error of at most 0.0003.
Values sent between devices are 32-bit elements; how exact they have to be, the bound alone decides.
A program may use at most 64 MiB of HBM per device.

```python
import jax
import jax.numpy as jnp
from jax import lax

D = 768
K = 256
BLOCKS = 4
R0 = 512
ROWS_DEV = 512
N = 131072


def pivot_rows_drawn(key):
    inner = jax.random.permutation(jax.random.fold_in(key, 17), N - 2)[:BLOCKS * K] + 1
    chosen = inner.reshape(BLOCKS, K).astype(jnp.int32)
    chosen = chosen.at[0, 0].set(N - 1)
    chosen = chosen.at[BLOCKS - 1, 0].set(0)
    return chosen


def draw_pivot_owner(key, part):
    return (pivot_rows_drawn(key) // ROWS_DEV).astype(jnp.int32)


def draw_pivot_local(key, part):
    return (pivot_rows_drawn(key) % ROWS_DEV).astype(jnp.int32)


def steps_of(stream_key, shape, cuts, smallest, largest):
    loudness = 1.0
    for position, blocks in cuts:
        steps = jax.random.uniform(jax.random.fold_in(jax.random.fold_in(stream_key, 6), position), (blocks,), jnp.float32, smallest / len(cuts), largest / len(cuts))
        loudness = loudness * jnp.repeat(jnp.exp(steps), shape[position] // blocks).reshape((-1,) + (1,) * (len(shape) - 1 - position))
    return loudness


def noise(rng, dims, deviation, bound, shards=(), kind=jnp.bfloat16):
    entries = deviation * jax.random.normal(rng, dims, jnp.float32)
    if shards:
        entries = entries * steps_of(rng, dims, shards, -0.22, 0.18)
    return jnp.clip(entries, -bound, bound).astype(kind)


def setup_inputs(seed: int = 0) -> dict:
    key_of = jax.random.split(jax.random.key(seed), 6)
    return {
        "embeddings": noise(key_of[0], (N, D), 0.036, 0.25, ((0, 256),)),
        "factor": noise(key_of[1], (N, R0), 0.02, 0.15, ((0, 256),), jnp.float32),
        "diagonal": jnp.clip(0.5 + 0.5 * jax.random.uniform(key_of[2], (N,), jnp.float32) ** steps_of(key_of[2], (N,), ((0, 256),), -0.2, 0.2), 0.5, 1.0),
        "pivot_owner": draw_pivot_owner(jax.random.fold_in(key_of[5], 71), 0),
        "pivot_local": draw_pivot_local(jax.random.fold_in(key_of[5], 71), 0),
    }


gamma_scale = 1.0
ridge_base = 0.5

def gauss_kernel(left, left_squares, right, right_squares):
    inner = jnp.dot(left.astype(jnp.float32), right.T.astype(jnp.float32), preferred_element_type=jnp.float32)
    return jnp.exp(-gamma_scale * (left_squares[:, None] + right_squares[None, :] - 2.0 * inner))

def gershgorin(pivot_gram):
    absolute = jnp.sum(jnp.abs(pivot_gram), axis=1) - jnp.abs(jnp.diagonal(pivot_gram))
    return ridge_base + jnp.maximum(jnp.max(absolute - jnp.diagonal(pivot_gram)), 0.0)

def reference(embeddings, factor, diagonal, pivot_owner, pivot_local):
    squares = jnp.sum(jnp.square(embeddings.astype(jnp.float32)), axis=1)
    columns = factor
    residual_diag = diagonal
    blocks_out = []
    for block in range(BLOCKS):
        chosen = (pivot_owner[block] * ROWS_DEV + pivot_local[block]).astype(jnp.int32)
        points = jnp.take(embeddings, chosen, axis=0)
        point_squares = jnp.take(squares, chosen, axis=0)
        factor_rows = jnp.take(columns, chosen, axis=0)
        kernel = gauss_kernel(embeddings, squares, points, point_squares)
        resid = kernel - jnp.dot(columns, factor_rows.T, precision=lax.Precision.HIGHEST)
        pivot_kernel = gauss_kernel(points, point_squares, points, point_squares)
        pivot_gram = pivot_kernel - jnp.dot(factor_rows, factor_rows.T, precision=lax.Precision.HIGHEST)
        pivot_gram = 0.5 * (pivot_gram + pivot_gram.T)
        shift = gershgorin(pivot_gram)
        lower = jnp.linalg.cholesky(pivot_gram + shift * jnp.eye(K, dtype=jnp.float32))
        solved = lax.linalg.triangular_solve(lower, resid.T, left_side=True, lower=True)
        block_cols = solved.T
        residual_diag = residual_diag - jnp.sum(block_cols * block_cols, axis=1)
        columns = jnp.concatenate([columns, block_cols], axis=1)
        blocks_out.append(block_cols)
    return (jnp.concatenate(blocks_out, axis=1), residual_diag)
```

```python
import functools
import jax
import jax.numpy as jnp
from jax import lax
from jax.experimental import pallas as pl
from jax.experimental.pallas import tpu as pltpu
from jax.sharding import PartitionSpec as P

ridge_base = 0.5
HALF = 128
NT = (((1,), (1,)), ((), ()))
NN = (((1,), (0,)), ((), ()))


def lane_splat(a, c):
    return jnp.broadcast_to(a[:, c : c + 1], (8, HALF))


def row_splat(a, r):
    return jnp.broadcast_to(a[r : r + 1, :], (8, HALF))


def inverse_factor(rows):
    sub = lax.broadcasted_iota(jnp.int32, (8, HALF), 0)
    lane = lax.broadcasted_iota(jnp.int32, (8, HALF), 1)
    rows = list(rows)
    groups = len(rows)
    out = []
    for g in range(groups):
        base = 8 * g
        split = [lane_splat(rows[g], base + k) for k in range(8)]
        inside = (lane >= base) & (lane < base + 8)
        start = jnp.where(inside, jnp.where(lane == sub + base, 1.0, 0.0), rows[g])
        solved, forward = start, start
        pivots = jnp.ones((8, HALF), jnp.float32)
        for j in range(8):
            pivot = row_splat(split[j], j)
            recip = 1.0 / pivot
            scaled = split[j] * recip
            factor = jnp.where(sub == j, 1.0 - recip, scaled)
            pivots = jnp.where(sub == j, pivot, pivots)
            for k in range(j + 1, 8):
                split[k] = split[k] - factor * row_splat(split[k], j)
            solved = solved - factor * row_splat(solved, j)
            if j < 7:
                forward = forward - jnp.where(sub > j, scaled, 0.0) * row_splat(forward, j)
        out.append(jnp.where(lane < base + 8, forward * lax.rsqrt(pivots), 0.0))
        if g + 1 < groups:
            spread = [row_splat(solved, k) for k in range(8)]
            for i in range(g + 1, groups):
                t = [lane_splat(rows[i], base + k) * spread[k] for k in range(8)]
                total = ((t[0] + t[1]) + (t[2] + t[3])) + ((t[4] + t[5]) + (t[6] + t[7]))
                rows[i] = jnp.where(inside, 0.0, rows[i]) - total
    return out


def dot_exact(a, b, dims):
    return lax.dot_general(
        a, b, dims, precision=lax.Precision.HIGHEST, preferred_element_type=jnp.float32
    )


def halves(a):
    high = a.astype(jnp.bfloat16)
    return high, (a - high.astype(jnp.float32)).astype(jnp.bfloat16)


def dot_split(a, b, dims):
    (a_hi, a_lo), (b_hi, b_lo) = a, b
    dot = functools.partial(
        lax.dot_general, dimension_numbers=dims, preferred_element_type=jnp.float32
    )
    return dot(a_hi, b_hi) + (dot(a_hi, b_lo) + dot(a_lo, b_hi))


def window_kernel(
    x_ref, f_ref, d_ref, p_ref, c_ref, nd_ref,
    g_ref, w_ref, m_ref, xb_ref, fhi_ref, flo_ref, fphi_ref, fplo_ref, sq_ref, sqp_ref,
):
    K = 2 * HALF
    width = x_ref.shape[1]
    n_piv = p_ref.shape[0]
    blocks = n_piv // K
    ones = jnp.ones((8, width), jnp.bfloat16)

    fhi_ref[...], flo_ref[...] = halves(f_ref[...])
    fphi_ref[...], fplo_ref[...] = halves(p_ref[:, width:])
    xb_ref[...] = p_ref[:, :width].astype(jnp.bfloat16)
    wide = x_ref[...].astype(jnp.float32)
    sq_ref[...] = jnp.sum(wide * wide, axis=1, keepdims=True)
    wide = p_ref[:, :width]
    sqp_ref[...] = jnp.sum(wide * wide, axis=1, keepdims=True)

    def residual(x, sq, f, xp, sq_row, fp):
        inner = lax.dot_general(x, xp, NT, preferred_element_type=jnp.float32)
        return jnp.exp(2.0 * inner - sq - sq_row) - dot_split(f, fp, NT)

    def column(b, _):
        at = pl.ds(pl.multiple_of(b * K, K), K)
        xp = xb_ref[at, :]
        points = p_ref[at, :width]
        sq_hi, sq_lo = halves(points * points)
        sq_row = lax.dot_general(ones, sq_hi, NT, preferred_element_type=jnp.float32)
        sq_row = sq_row + lax.dot_general(ones, sq_lo, NT, preferred_element_type=jnp.float32)
        sq_row = sq_row[0:1, :]
        fp = (fphi_ref[at, :], fplo_ref[at, :])
        c_ref[:, at] = residual(
            x_ref[...], sq_ref[...], (fhi_ref[...], flo_ref[...]), xp, sq_row, fp
        )

        def below(r, _):
            to = pl.ds(pl.multiple_of(r * K, K), K)
            g_ref[to, at] = residual(
                xb_ref[to, :], sqp_ref[to, :], (fphi_ref[to, :], fplo_ref[to, :]), xp, sq_row, fp
            )
            return 0

        lax.fori_loop(b, blocks, below, 0)
        return 0

    lax.fori_loop(0, blocks, column, 0)

    eye = lax.broadcasted_iota(jnp.int32, (K, K), 0) == lax.broadcasted_iota(jnp.int32, (K, K), 1)

    def factor_half(start):
        rows = [w_ref[pl.ds(start + 8 * i, 8), start : start + HALF] for i in range(HALF // 8)]
        for i, row in enumerate(inverse_factor(rows)):
            w_ref[pl.ds(start + 8 * i, 8), start : start + HALF] = row

    def block(b, total):
        at = pl.ds(pl.multiple_of(b * K, K), K)
        gram = g_ref[at, at]
        diag = jnp.sum(jnp.where(eye, gram, 0.0), axis=0, keepdims=True)
        off = jnp.sum(jnp.abs(gram), axis=0, keepdims=True) - jnp.abs(diag)
        shift = ridge_base + jnp.maximum(jnp.max(off - diag, axis=1, keepdims=True), 0.0)
        w_ref[...] = gram + jnp.where(eye, shift, 0.0)

        factor_half(0)
        first = w_ref[:HALF, :HALF]
        low = dot_exact(w_ref[HALF:, :HALF], first, NT)
        w_ref[HALF:, HALF:] = w_ref[HALF:, HALF:] - dot_exact(low, low, NT)
        carried = dot_exact(low, first, NN)
        factor_half(HALF)
        w_ref[HALF:, :HALF] = -dot_exact(w_ref[HALF:, HALF:], carried, NN)
        w_ref[:HALF, HALF:] = jnp.zeros((HALF, HALF), jnp.float32)
        inverse = halves(w_ref[...])

        cols = dot_split(halves(c_ref[:, at]), inverse, NT)
        c_ref[:, at] = cols
        cols_split = halves(cols)
        squared = cols * cols
        total = total + squared[:, :HALF] + squared[:, HALF:]

        def panel(r, _):
            to = pl.ds(pl.multiple_of(r * K, K), K)
            m_ref[to, :] = dot_split(halves(g_ref[to, at]), inverse, NT)
            return 0

        def trail(c, _):
            to = pl.ds(pl.multiple_of(c * K, K), K)
            right = halves(m_ref[to, :])
            c_ref[:, to] = c_ref[:, to] - dot_split(cols_split, right, NT)

            def trail_rows(r, _):
                row = pl.ds(pl.multiple_of(r * K, K), K)
                g_ref[row, to] = g_ref[row, to] - dot_split(halves(m_ref[row, :]), right, NT)
                return 0

            lax.fori_loop(c, blocks, trail_rows, 0)
            return 0

        lax.fori_loop(b + 1, blocks, panel, 0)
        lax.fori_loop(b + 1, blocks, trail, 0)
        return total

    total = lax.fori_loop(0, blocks, block, jnp.zeros((x_ref.shape[0], HALF), jnp.float32))
    sums = dot_exact(jnp.ones((8, HALF), jnp.float32), total, NT)
    nd_ref[...] = d_ref[...] - sums[0:1, :]


def window(x, f, diag, gathered):
    rows, width = x.shape
    rank = f.shape[1]
    n_piv = gathered.shape[0]
    K = 2 * HALF
    cols, new_diag = pl.pallas_call(
        window_kernel,
        out_shape=(
            jax.ShapeDtypeStruct((rows, n_piv), jnp.float32),
            jax.ShapeDtypeStruct((1, rows), jnp.float32),
        ),
        in_specs=[pl.BlockSpec(memory_space=pltpu.VMEM)] * 4,
        out_specs=[pl.BlockSpec(memory_space=pltpu.VMEM)] * 2,
        scratch_shapes=[
            pltpu.VMEM((n_piv, n_piv), jnp.float32),
            pltpu.VMEM((K, K), jnp.float32),
            pltpu.VMEM((n_piv, K), jnp.float32),
            pltpu.VMEM((n_piv, width), jnp.bfloat16),
            pltpu.VMEM((rows, rank), jnp.bfloat16),
            pltpu.VMEM((rows, rank), jnp.bfloat16),
            pltpu.VMEM((n_piv, rank), jnp.bfloat16),
            pltpu.VMEM((n_piv, rank), jnp.bfloat16),
            pltpu.VMEM((rows, 1), jnp.float32),
            pltpu.VMEM((n_piv, 1), jnp.float32),
        ],
        compiler_params=pltpu.CompilerParams(vmem_limit_bytes=56 << 20),
        name="window",
    )(x, f, diag.reshape(1, rows), gathered)
    return cols, new_diag.reshape(rows)
MESH = pl.DeviceIdType.MESH
X, Y, Z = 4, 4, 8


def gather_kernel(s_ref, out_ref, sib, near1, near2, near3, send, recv):
    n_piv, width = s_ref.shape
    half, piece1, piece2, piece3, cut = (
        n_piv // 2, n_piv // 2 // X, n_piv // 2 // X // Y, 8, width // 2,
    )
    where = lax.axis_index("rows")
    x = lax.axis_index("sub")
    core = where % 2
    y = (where // 2) % Y
    z = where // (2 * Y)
    p1 = x * (1 - core) + y * core
    p2 = y * (1 - core) + x * core

    def device(q1, q2, qz):
        qx = q1 * (1 - core) + q2 * core
        qy = q2 * (1 - core) + q1 * core
        return ((qz * Y + qy) * 2 + core, qx)

    sibling = ((z * Y + y) * 2 + 1 - core, x)
    right1, left1 = device((p1 + 1) % X, p2, z), device((p1 + 3) % X, p2, z)
    right2, left2 = device(p1, (p2 + 1) % Y, z), device(p1, (p2 + 3) % Y, z)
    along_z = [device(p1, p2, (z + d) % Z) for d in range(1, Z)]

    barrier = pltpu.get_barrier_semaphore()
    partners = [sibling, right1, left1, right2, left2] + along_z
    for partner in partners:
        pl.semaphore_signal(barrier, inc=1, device_id=partner, device_id_type=MESH)
    pl.semaphore_wait(barrier, len(partners))

    started = []

    def copy(src, dst, target):
        k = len(started)
        made = pltpu.make_async_remote_copy(
            src_ref=src, dst_ref=dst, send_sem=send.at[k], recv_sem=recv.at[k],
            device_id=target, device_id_type=MESH,
        )
        made.start()
        started.append(made)
        return made

    def span(start, size):
        return pl.ds(pl.multiple_of(start, 8), size)

    order = (2, 1, 3, 0)
    from_sibling = {}
    for d in order:
        q = (p2 + d) % X
        from_sibling[d] = copy(
            s_ref.at[span((1 - core) * half + q * piece1, piece1), :],
            sib.at[span(q * piece1, piece1), :],
            sibling,
        )

    def merge(d):
        q = (p1 + d) % X
        from_sibling[d].wait_recv()
        at = span(q * piece1, piece1)
        sib[at, :] = sib[at, :] + s_ref[span(core * half + q * piece1, piece1), :]

    def scatter(base, piece, p, right, left, near, ready):
        hp = piece // 2

        def rows(d, part):
            return span(base + ((p + d) % 4) * piece + part * hp, hp)

        ready(2)
        over_right = copy(sib.at[rows(2, 0), :], near.at[0], right)
        over_left = copy(sib.at[rows(2, 1), :], near.at[1], left)
        ready(1)
        plain_right = copy(sib.at[rows(1, 1), :], near.at[2], right)
        ready(3)
        plain_left = copy(sib.at[rows(3, 0), :], near.at[3], left)
        ready(0)
        over_right.wait_recv()
        sib[rows(1, 0), :] = sib[rows(1, 0), :] + near[0]
        last_right = copy(sib.at[rows(1, 0), :], near.at[4], right)
        over_left.wait_recv()
        sib[rows(3, 1), :] = sib[rows(3, 1), :] + near[1]
        last_left = copy(sib.at[rows(3, 1), :], near.at[5], left)
        plain_right.wait_recv()
        sib[rows(0, 1), :] = sib[rows(0, 1), :] + near[2]
        plain_left.wait_recv()
        sib[rows(0, 0), :] = sib[rows(0, 0), :] + near[3]
        last_right.wait_recv()
        sib[rows(0, 0), :] = sib[rows(0, 0), :] + near[4]
        last_left.wait_recv()
        sib[rows(0, 1), :] = sib[rows(0, 1), :] + near[5]

    scatter(0, piece1, p1, right1, left1, near1, merge)
    base2 = p1 * piece1
    scatter(base2, piece2, p2, right2, left2, near2, lambda d: None)
    base3 = base2 + p2 * piece2

    def cell(base, q):
        return span(base + (q // 2) * piece3, piece3), pl.ds(
            pl.multiple_of((q % 2) * cut, 128), cut
        )

    arriving = []
    for d in range(1, Z):
        arriving.append(copy(sib.at[cell(base3, (z + d) % Z)], near3.at[d - 1], along_z[d - 1]))
    total = sib[cell(base3, z)]
    for d in range(1, Z):
        arriving[d - 1].wait_recv()
        total = total + near3[d - 1]
    out3 = core * half + base3
    mine = cell(out3, z)
    out_ref[mine] = total
    arriving = [copy(out_ref.at[mine], out_ref.at[mine], along_z[d - 1]) for d in range(1, Z)]
    for made in arriving:
        made.wait_recv()

    def gather(base, piece, p, right, left, done):
        hp = piece // 2

        def rows(d, part, size):
            return span(base + ((p + d) % 4) * piece + part * hp, size)

        own = out_ref.at[rows(0, 0, piece), :]
        from_left = copy(own, own, right)
        from_right = copy(own, own, left)
        done(rows(0, 0, piece))
        from_left.wait_recv()
        on = out_ref.at[rows(3, 0, hp), :]
        far_left = copy(on, on, right)
        done(rows(3, 0, piece))
        from_right.wait_recv()
        on = out_ref.at[rows(1, 1, hp), :]
        far_right = copy(on, on, left)
        done(rows(1, 0, piece))
        far_left.wait_recv()
        done(rows(2, 0, hp))
        far_right.wait_recv()
        done(rows(2, 1, hp))

    gather(core * half + base2, piece2, p2, right2, left2, lambda at: None)
    across = []

    def hand_over(at):
        across.append(copy(out_ref.at[at, :], out_ref.at[at, :], sibling))

    gather(core * half, piece1, p1, right1, left1, hand_over)
    for made in across:
        made.wait_recv()
    for made in started:
        made.wait_send()


COPIES = 4 + 6 + 6 + 7 + 7 + 4 + 4 + 5


def gather_rows(contribution):
    n_piv, width = contribution.shape
    half = n_piv // 2
    return pl.pallas_call(
        gather_kernel,
        out_shape=jax.ShapeDtypeStruct((n_piv, width), jnp.float32),
        in_specs=[pl.BlockSpec(memory_space=pltpu.VMEM)],
        out_specs=pl.BlockSpec(memory_space=pltpu.VMEM),
        scratch_shapes=[
            pltpu.VMEM((half, width), jnp.float32),
            pltpu.VMEM((6, half // X // 2, width), jnp.float32),
            pltpu.VMEM((6, half // X // Y // 2, width), jnp.float32),
            pltpu.VMEM((Z - 1, 8, width // 2), jnp.float32),
            pltpu.SemaphoreType.DMA((COPIES,)),
            pltpu.SemaphoreType.DMA((COPIES,)),
        ],
        compiler_params=pltpu.CompilerParams(
            collective_id=0, has_side_effects=True, vmem_limit_bytes=40 << 20
        ),
        name="gather_rows",
    )(contribution)


def on_device(embeddings, factor, diagonal, pivot_owner, pivot_local):
    local_rows = embeddings.shape[0]
    owners = pivot_owner.reshape(-1)
    places = pivot_local.reshape(-1)
    device = lax.axis_index("rows") * lax.axis_size("sub") + lax.axis_index("sub")
    positions = lax.broadcasted_iota(jnp.int32, (owners.shape[0], local_rows), 1)
    select = ((owners[:, None] == device) & (places[:, None] == positions)).astype(jnp.float32)
    points = jnp.dot(
        select.astype(jnp.bfloat16), embeddings, preferred_element_type=jnp.float32
    )
    factor_rows = jnp.dot(select, factor, precision=lax.Precision.HIGHEST)
    gathered = gather_rows(jnp.concatenate([points, factor_rows], axis=1))
    return window(embeddings, factor, diagonal, gathered)


def solution(mesh):
    return jax.shard_map(
        on_device,
        mesh=mesh,
        in_specs=(P(("rows", "sub"), None), P(("rows", "sub"), None), P(("rows", "sub")), P(), P()),
        out_specs=(P(("rows", "sub"), None), P(("rows", "sub"))),
        check_vma=False,
    )
```

```python
import functools
import jax
import jax.numpy as jnp
from jax import lax
from jax.experimental import pallas as pl
from jax.experimental.pallas import tpu as pltpu
from jax.sharding import PartitionSpec as P

ridge_base = 0.5
HALF = 128
NT = (((1,), (1,)), ((), ()))
NN = (((1,), (0,)), ((), ()))


def lane_splat(a, c):
    return jnp.broadcast_to(a[:, c : c + 1], (8, HALF))


def inverse_factor(rows, spare):
    sub = lax.broadcasted_iota(jnp.int32, (8, HALF), 0)
    lane = lax.broadcasted_iota(jnp.int32, (8, HALF), 1)
    rows = list(rows)
    groups = len(rows)
    near = 2
    out = []
    for g in range(groups):
        base = 8 * g

        def splats(value, slot, which):
            start = (g % 2) * 72 + 8 * slot
            spare[start : start + 8, :] = value
            return [jnp.broadcast_to(spare[start + k : start + k + 1, :], (8, HALF)) for k in which]

        inside = (lane >= base) & (lane < base + 8)
        start = jnp.where(inside, jnp.where(lane == sub + base, 1.0, 0.0), rows[g])
        a = [splats(lane_splat(rows[g], base + c), c, range(c + 1)) for c in range(8)]
        y = splats(start, 8, range(8))
        inverses, factors, pivots, forward = [], [], [], []
        for j in range(0, 8, 2):
            p, q, r = a[j][j], a[j + 1][j], a[j + 1][j + 1]
            det = p * r - q * q
            recip = 1.0 / det
            first = 1.0 / p
            pivots += [p, det * first]
            forward += [y[j], y[j + 1] - (q * first) * y[j]]
            inverses.append((r * recip, q * recip, p * recip))
            factor = {
                c: ((a[c][j] * r - a[c][j + 1] * q) * recip, (a[c][j + 1] * p - a[c][j] * q) * recip)
                for c in range(j + 2, 8)
            }
            factors.append(factor)
            for k in range(j + 2, 8):
                for c in range(k, 8):
                    a[c][k] = a[c][k] - (factor[k][0] * a[c][j] + factor[k][1] * a[c][j + 1])
                y[k] = y[k] - (factor[k][0] * y[j] + factor[k][1] * y[j + 1])
        done, scale = forward[0], pivots[0]
        for k in range(1, 8):
            done = jnp.where(sub == k, forward[k], done)
            scale = jnp.where(sub == k, pivots[k], scale)
        out.append(jnp.where(lane < base + 8, done * lax.rsqrt(scale), 0.0))
        solved = [None] * 8
        for j in (6, 4, 2, 0):
            left, cross, right = inverses[j // 2]
            top = left * y[j] - cross * y[j + 1]
            bottom = right * y[j + 1] - cross * y[j]
            for k in range(j + 2, 8):
                top = top - factors[j // 2][k][0] * solved[k]
                bottom = bottom - factors[j // 2][k][1] * solved[k]
            solved[j], solved[j + 1] = top, bottom
        for i in range(g + 1, min(groups, g + 1 + near)):
            t = [lane_splat(rows[i], base + k) * solved[k] for k in range(8)]
            total = ((t[0] + t[1]) + (t[2] + t[3])) + ((t[4] + t[5]) + (t[6] + t[7]))
            rows[i] = jnp.where(inside, 0.0, rows[i]) - total
        if g + 1 + near < groups:
            merged = solved[0]
            for k in range(1, 8):
                merged = jnp.where(sub == k, solved[k], merged)
            zero = jnp.zeros((8, HALF), jnp.float32)
            weights = jnp.concatenate([merged if k == g else zero for k in range(groups)], axis=0)
            change = dot_exact(jnp.concatenate(rows[g + 1 + near :], axis=0), weights, NN)
            for k, i in enumerate(range(g + 1 + near, groups)):
                rows[i] = jnp.where(inside, 0.0, rows[i]) - change[8 * k : 8 * k + 8]
    return out


def dot_exact(a, b, dims):
    return lax.dot_general(
        a, b, dims, precision=lax.Precision.HIGHEST, preferred_element_type=jnp.float32
    )


def halves(a):
    high = a.astype(jnp.bfloat16)
    return high, (a - high.astype(jnp.float32)).astype(jnp.bfloat16)


def dot_split(a, b, dims):
    (a_hi, a_lo), (b_hi, b_lo) = a, b
    dot = functools.partial(
        lax.dot_general, dimension_numbers=dims, preferred_element_type=jnp.float32
    )
    return dot(a_hi, b_hi) + (dot(a_hi, b_lo) + dot(a_lo, b_hi))


def window_kernel(
    x_ref, f_ref, d_ref, xp_ref, fp_ref, c_ref, nd_ref,
    g_ref, w_ref, m_ref, xb_ref, fhi_ref, flo_ref, fphi_ref, fplo_ref, sq_ref, sqp_ref, spare_ref,
):
    K = 2 * HALF
    n_piv = xp_ref.shape[0]
    blocks = n_piv // K
    ones = jnp.ones((8, x_ref.shape[1]), jnp.bfloat16)

    fhi_ref[...], flo_ref[...] = halves(f_ref[...])
    fphi_ref[...], fplo_ref[...] = halves(fp_ref[...])
    xb_ref[...] = xp_ref[...].astype(jnp.bfloat16)
    wide = x_ref[...].astype(jnp.float32)
    sq_ref[...] = jnp.sum(wide * wide, axis=1, keepdims=True)
    wide = xp_ref[...]
    sqp_ref[...] = jnp.sum(wide * wide, axis=1, keepdims=True)

    def residual(x, sq, f, xp, sq_row, fp):
        inner = lax.dot_general(x, xp, NT, preferred_element_type=jnp.float32)
        return jnp.exp(2.0 * inner - sq - sq_row) - dot_split(f, fp, NT)

    def column(b, _):
        at = pl.ds(pl.multiple_of(b * K, K), K)
        xp = xb_ref[at, :]
        points = xp_ref[at, :]
        sq_hi, sq_lo = halves(points * points)
        sq_row = lax.dot_general(ones, sq_hi, NT, preferred_element_type=jnp.float32)
        sq_row = sq_row + lax.dot_general(ones, sq_lo, NT, preferred_element_type=jnp.float32)
        sq_row = sq_row[0:1, :]
        fp = (fphi_ref[at, :], fplo_ref[at, :])
        c_ref[:, at] = residual(
            x_ref[...], sq_ref[...], (fhi_ref[...], flo_ref[...]), xp, sq_row, fp
        )

        def below(r, _):
            to = pl.ds(pl.multiple_of(r * K, K), K)
            g_ref[to, at] = residual(
                xb_ref[to, :], sqp_ref[to, :], (fphi_ref[to, :], fplo_ref[to, :]), xp, sq_row, fp
            )
            return 0

        lax.fori_loop(b, blocks, below, 0)
        return 0

    lax.fori_loop(0, blocks, column, 0)

    eye = lax.broadcasted_iota(jnp.int32, (K, K), 0) == lax.broadcasted_iota(jnp.int32, (K, K), 1)

    def factor_half(start):
        rows = [w_ref[pl.ds(start + 8 * i, 8), start : start + HALF] for i in range(HALF // 8)]
        for i, row in enumerate(inverse_factor(rows, spare_ref)):
            w_ref[pl.ds(start + 8 * i, 8), start : start + HALF] = row

    def block(b, total):
        at = pl.ds(pl.multiple_of(b * K, K), K)
        gram = g_ref[at, at]
        diag = jnp.sum(jnp.where(eye, gram, 0.0), axis=0, keepdims=True)
        off = jnp.sum(jnp.abs(gram), axis=0, keepdims=True) - jnp.abs(diag)
        shift = ridge_base + jnp.maximum(jnp.max(off - diag, axis=1, keepdims=True), 0.0)
        w_ref[...] = gram + jnp.where(eye, shift, 0.0)

        factor_half(0)
        first = w_ref[:HALF, :HALF]
        low = dot_exact(w_ref[HALF:, :HALF], first, NT)
        w_ref[HALF:, HALF:] = w_ref[HALF:, HALF:] - dot_exact(low, low, NT)
        carried = dot_exact(low, first, NN)
        factor_half(HALF)
        w_ref[HALF:, :HALF] = -dot_exact(w_ref[HALF:, HALF:], carried, NN)
        w_ref[:HALF, HALF:] = jnp.zeros((HALF, HALF), jnp.float32)
        inverse = halves(w_ref[...])

        cols = dot_split(halves(c_ref[:, at]), inverse, NT)
        c_ref[:, at] = cols
        cols_split = halves(cols)
        squared = cols * cols
        total = total + squared[:, :HALF] + squared[:, HALF:]

        def panel(r, _):
            to = pl.ds(pl.multiple_of(r * K, K), K)
            m_ref[to, :] = dot_split(halves(g_ref[to, at]), inverse, NT)
            return 0

        def trail(c, _):
            to = pl.ds(pl.multiple_of(c * K, K), K)
            right = halves(m_ref[to, :])
            c_ref[:, to] = c_ref[:, to] - dot_split(cols_split, right, NT)

            def trail_rows(r, _):
                row = pl.ds(pl.multiple_of(r * K, K), K)
                g_ref[row, to] = g_ref[row, to] - dot_split(halves(m_ref[row, :]), right, NT)
                return 0

            lax.fori_loop(c, blocks, trail_rows, 0)
            return 0

        lax.fori_loop(b + 1, blocks, panel, 0)
        lax.fori_loop(b + 1, blocks, trail, 0)
        return total

    total = lax.fori_loop(0, blocks, block, jnp.zeros((x_ref.shape[0], HALF), jnp.float32))
    sums = dot_exact(jnp.ones((8, HALF), jnp.float32), total, NT)
    nd_ref[...] = d_ref[...] - sums[0:1, :]


def window(x, f, diag, xp, fp):
    rows, width = x.shape
    rank = f.shape[1]
    n_piv = xp.shape[0]
    K = 2 * HALF
    cols, new_diag = pl.pallas_call(
        window_kernel,
        out_shape=(
            jax.ShapeDtypeStruct((rows, n_piv), jnp.float32),
            jax.ShapeDtypeStruct((1, rows), jnp.float32),
        ),
        in_specs=[pl.BlockSpec(memory_space=pltpu.VMEM)] * 5,
        out_specs=[pl.BlockSpec(memory_space=pltpu.VMEM)] * 2,
        scratch_shapes=[
            pltpu.VMEM((n_piv, n_piv), jnp.float32),
            pltpu.VMEM((K, K), jnp.float32),
            pltpu.VMEM((n_piv, K), jnp.float32),
            pltpu.VMEM((n_piv, width), jnp.bfloat16),
            pltpu.VMEM((rows, rank), jnp.bfloat16),
            pltpu.VMEM((rows, rank), jnp.bfloat16),
            pltpu.VMEM((n_piv, rank), jnp.bfloat16),
            pltpu.VMEM((n_piv, rank), jnp.bfloat16),
            pltpu.VMEM((rows, 1), jnp.float32),
            pltpu.VMEM((n_piv, 1), jnp.float32),
            pltpu.VMEM((144, HALF), jnp.float32),
        ],
        compiler_params=pltpu.CompilerParams(vmem_limit_bytes=56 << 20),
        name="window",
    )(x, f, diag.reshape(1, rows), xp, fp)
    return cols, new_diag.reshape(rows)
MESH = pl.DeviceIdType.MESH
X, Y, Z = 4, 4, 8


COPIES = 4 + 6 + 6 + 7 + 7 + 4 + 4 + 5


def gather_kernel(*refs):
    n_lanes = (len(refs) - 2) // 6
    send, recv = refs[-2:]
    where = lax.axis_index("rows")
    x = lax.axis_index("sub")
    core = where % 2
    y = (where // 2) % Y
    z = where // (2 * Y)
    p1 = x * (1 - core) + y * core
    p2 = y * (1 - core) + x * core

    def device(q1, q2, qz):
        qx = q1 * (1 - core) + q2 * core
        qy = q2 * (1 - core) + q1 * core
        return ((qz * Y + qy) * 2 + core, qx)

    sibling = ((z * Y + y) * 2 + 1 - core, x)
    right1, left1 = device((p1 + 1) % X, p2, z), device((p1 + 3) % X, p2, z)
    right2, left2 = device(p1, (p2 + 1) % Y, z), device(p1, (p2 + 3) % Y, z)
    along_z = [device(p1, p2, (z + d) % Z) for d in range(1, Z)]

    barrier = pltpu.get_barrier_semaphore()
    partners = [sibling, right1, left1, right2, left2] + along_z
    for partner in partners:
        pl.semaphore_signal(barrier, inc=1, device_id=partner, device_id_type=MESH)
    pl.semaphore_wait(barrier, len(partners))

    started = []

    def copy(src, dst, target):
        k = len(started)
        made = pltpu.make_async_remote_copy(
            src_ref=src, dst_ref=dst, send_sem=send.at[k], recv_sem=recv.at[k],
            device_id=target, device_id_type=MESH,
        )
        made.start()
        started.append(made)
        return made

    def span(start, size):
        return pl.ds(pl.multiple_of(start, 8), size)

    def travel(s_ref, out_ref, sib, near1, near2, near3):
        n_piv, width = s_ref.shape
        half = n_piv // 2
        piece1, piece2, piece3 = half // X, half // X // Y, 8
        cut = width // 2

        order = (2, 1, 3, 0)
        from_sibling = {}
        for d in order:
            q = (p2 + d) % X
            from_sibling[d] = copy(
                s_ref.at[span((1 - core) * half + q * piece1, piece1), :],
                sib.at[span(q * piece1, piece1), :],
                sibling,
            )
        yield

        def merge(d):
            q = (p1 + d) % X
            from_sibling[d].wait_recv()
            at = span(q * piece1, piece1)
            sib[at, :] = sib[at, :] + s_ref[span(core * half + q * piece1, piece1), :]

        def scatter(base, piece, p, right, left, near, ready):
            hp = piece // 2

            def rows(d, part):
                return span(base + ((p + d) % 4) * piece + part * hp, hp)

            ready(2)
            over_right = copy(sib.at[rows(2, 0), :], near.at[0], right)
            over_left = copy(sib.at[rows(2, 1), :], near.at[1], left)
            ready(1)
            plain_right = copy(sib.at[rows(1, 1), :], near.at[2], right)
            ready(3)
            plain_left = copy(sib.at[rows(3, 0), :], near.at[3], left)
            ready(0)
            yield
            over_right.wait_recv()
            sib[rows(1, 0), :] = sib[rows(1, 0), :] + near[0]
            last_right = copy(sib.at[rows(1, 0), :], near.at[4], right)
            over_left.wait_recv()
            sib[rows(3, 1), :] = sib[rows(3, 1), :] + near[1]
            last_left = copy(sib.at[rows(3, 1), :], near.at[5], left)
            yield
            plain_right.wait_recv()
            sib[rows(0, 1), :] = sib[rows(0, 1), :] + near[2]
            plain_left.wait_recv()
            sib[rows(0, 0), :] = sib[rows(0, 0), :] + near[3]
            last_right.wait_recv()
            sib[rows(0, 0), :] = sib[rows(0, 0), :] + near[4]
            last_left.wait_recv()
            sib[rows(0, 1), :] = sib[rows(0, 1), :] + near[5]

        yield from scatter(0, piece1, p1, right1, left1, near1, merge)
        base2 = p1 * piece1
        yield from scatter(base2, piece2, p2, right2, left2, near2, lambda d: None)
        base3 = base2 + p2 * piece2

        def cell(base, q):
            return span(base + (q // 2) * piece3, piece3), pl.ds(
                pl.multiple_of((q % 2) * cut, 128), cut
            )

        arriving = []
        for d in range(1, Z):
            arriving.append(
                copy(sib.at[cell(base3, (z + d) % Z)], near3.at[d - 1], along_z[d - 1])
            )
        yield
        total = sib[cell(base3, z)]
        for d in range(1, Z):
            arriving[d - 1].wait_recv()
            total = total + near3[d - 1]
        mine = cell(core * half + base3, z)
        out_ref[mine] = total
        arriving = [
            copy(out_ref.at[mine], out_ref.at[mine], along_z[d - 1]) for d in range(1, Z)
        ]
        yield
        for made in arriving:
            made.wait_recv()

        def gather(base, piece, p, right, left, done):
            hp = piece // 2

            def rows(d, part, size):
                return span(base + ((p + d) % 4) * piece + part * hp, size)

            own = out_ref.at[rows(0, 0, piece), :]
            from_left = copy(own, own, right)
            from_right = copy(own, own, left)
            done(rows(0, 0, piece))
            yield
            from_left.wait_recv()
            on = out_ref.at[rows(3, 0, hp), :]
            far_left = copy(on, on, right)
            done(rows(3, 0, piece))
            from_right.wait_recv()
            on = out_ref.at[rows(1, 1, hp), :]
            far_right = copy(on, on, left)
            done(rows(1, 0, piece))
            yield
            far_left.wait_recv()
            done(rows(2, 0, hp))
            far_right.wait_recv()
            done(rows(2, 1, hp))

        yield from gather(core * half + base2, piece2, p2, right2, left2, lambda at: None)
        across = []

        def hand_over(at):
            across.append(copy(out_ref.at[at, :], out_ref.at[at, :], sibling))

        yield from gather(core * half, piece1, p1, right1, left1, hand_over)
        yield
        for made in across:
            made.wait_recv()

    ins, outs, scratch = refs[:n_lanes], refs[n_lanes : 2 * n_lanes], refs[2 * n_lanes : -2]
    ways = [
        travel(ins[i], outs[i], *scratch[4 * i : 4 * i + 4]) for i in range(n_lanes)
    ]
    while ways:
        ways = [way for way in ways if next(way, True) is None]
    for made in started:
        made.wait_send()


def gather_rows(*parts):
    scratch = []
    for part in parts:
        n_piv, width = part.shape
        half = n_piv // 2
        scratch += [
            pltpu.VMEM((half, width), jnp.float32),
            pltpu.VMEM((6, half // X // 2, width), jnp.float32),
            pltpu.VMEM((6, half // X // Y // 2, width), jnp.float32),
            pltpu.VMEM((Z - 1, 8, width // 2), jnp.float32),
        ]
    copies = COPIES * len(parts)
    return pl.pallas_call(
        gather_kernel,
        out_shape=tuple(jax.ShapeDtypeStruct(part.shape, jnp.float32) for part in parts),
        in_specs=[pl.BlockSpec(memory_space=pltpu.VMEM)] * len(parts),
        out_specs=[pl.BlockSpec(memory_space=pltpu.VMEM)] * len(parts),
        scratch_shapes=scratch
        + [pltpu.SemaphoreType.DMA((copies,)), pltpu.SemaphoreType.DMA((copies,))],
        compiler_params=pltpu.CompilerParams(
            collective_id=0, has_side_effects=True, vmem_limit_bytes=40 << 20
        ),
        name="gather_rows",
    )(*parts)


def on_device(embeddings, factor, diagonal, pivot_owner, pivot_local):
    local_rows = embeddings.shape[0]
    owners = pivot_owner.reshape(-1)
    places = pivot_local.reshape(-1)
    device = lax.axis_index("rows") * lax.axis_size("sub") + lax.axis_index("sub")
    positions = lax.broadcasted_iota(jnp.int32, (owners.shape[0], local_rows), 1)
    select = ((owners[:, None] == device) & (places[:, None] == positions)).astype(jnp.float32)
    points = jnp.dot(
        select.astype(jnp.bfloat16), embeddings, preferred_element_type=jnp.float32
    )
    factor_rows = jnp.dot(select, factor, precision=lax.Precision.HIGHEST)
    points, factor_rows = gather_rows(points, factor_rows)
    return window(embeddings, factor, diagonal, points, factor_rows)


def solution(mesh):
    return jax.shard_map(
        on_device,
        mesh=mesh,
        in_specs=(P(("rows", "sub"), None), P(("rows", "sub"), None), P(("rows", "sub")), P(), P()),
        out_specs=(P(("rows", "sub"), None), P(("rows", "sub"))),
        check_vma=False,
    )
```

```python
import functools
import jax
import jax.numpy as jnp
from jax import lax
from jax.experimental import pallas as pl
from jax.experimental.pallas import tpu as pltpu
from jax.sharding import PartitionSpec as P

ridge_base = 0.5
HALF = 128
NT = (((1,), (1,)), ((), ()))
NN = (((1,), (0,)), ((), ()))


def lane_splat(a, c):
    return jnp.broadcast_to(a[:, c : c + 1], (8, HALF))


def inverse_factor(rows, spare):
    sub = lax.broadcasted_iota(jnp.int32, (8, HALF), 0)
    lane = lax.broadcasted_iota(jnp.int32, (8, HALF), 1)
    rows = list(rows)
    groups = len(rows)
    near = 2
    out = []
    for g in range(groups):
        base = 8 * g

        def splats(value, slot, which):
            start = (g % 2) * 72 + 8 * slot
            spare[start : start + 8, :] = value
            return [jnp.broadcast_to(spare[start + k : start + k + 1, :], (8, HALF)) for k in which]

        inside = (lane >= base) & (lane < base + 8)
        start = jnp.where(inside, jnp.where(lane == sub + base, 1.0, 0.0), rows[g])
        a = [splats(lane_splat(rows[g], base + c), c, range(c + 1)) for c in range(8)]
        y = splats(start, 8, range(8))
        inverses, factors, pivots, forward = [], [], [], []
        for j in range(0, 8, 2):
            p, q, r = a[j][j], a[j + 1][j], a[j + 1][j + 1]
            det = p * r - q * q
            recip = 1.0 / det
            first = 1.0 / p
            pivots += [p, det * first]
            forward += [y[j], y[j + 1] - (q * first) * y[j]]
            inverses.append((r * recip, q * recip, p * recip))
            factor = {
                c: ((a[c][j] * r - a[c][j + 1] * q) * recip, (a[c][j + 1] * p - a[c][j] * q) * recip)
                for c in range(j + 2, 8)
            }
            factors.append(factor)
            for k in range(j + 2, 8):
                for c in range(k, 8):
                    a[c][k] = a[c][k] - (factor[k][0] * a[c][j] + factor[k][1] * a[c][j + 1])
                y[k] = y[k] - (factor[k][0] * y[j] + factor[k][1] * y[j + 1])
        done, scale = forward[0], pivots[0]
        for k in range(1, 8):
            done = jnp.where(sub == k, forward[k], done)
            scale = jnp.where(sub == k, pivots[k], scale)
        out.append(jnp.where(lane < base + 8, done * lax.rsqrt(scale), 0.0))
        solved = [None] * 8
        for j in (6, 4, 2, 0):
            left, cross, right = inverses[j // 2]
            top = left * y[j] - cross * y[j + 1]
            bottom = right * y[j + 1] - cross * y[j]
            for k in range(7, j + 1, -1):
                top = top - factors[j // 2][k][0] * solved[k]
                bottom = bottom - factors[j // 2][k][1] * solved[k]
            solved[j], solved[j + 1] = top, bottom
        for i in range(g + 1, min(groups, g + 1 + near)):
            t = [lane_splat(rows[i], base + k) * solved[k] for k in range(8)]
            total = ((t[0] + t[1]) + (t[2] + t[3])) + ((t[4] + t[5]) + (t[6] + t[7]))
            rows[i] = jnp.where(inside, 0.0, rows[i]) - total
        if g + 1 + near < groups:
            merged = solved[0]
            for k in range(1, 8):
                merged = jnp.where(sub == k, solved[k], merged)
            zero = jnp.zeros((8, HALF), jnp.float32)
            weights = jnp.concatenate([merged if k == g else zero for k in range(groups)], axis=0)
            change = dot_exact(jnp.concatenate(rows[g + 1 + near :], axis=0), weights, NN)
            for k, i in enumerate(range(g + 1 + near, groups)):
                rows[i] = jnp.where(inside, 0.0, rows[i]) - change[8 * k : 8 * k + 8]
    return out


def dot_exact(a, b, dims):
    return lax.dot_general(
        a, b, dims, precision=lax.Precision.HIGHEST, preferred_element_type=jnp.float32
    )


def halves(a):
    high = a.astype(jnp.bfloat16)
    return high, (a - high.astype(jnp.float32)).astype(jnp.bfloat16)


def dot_split(a, b, dims):
    (a_hi, a_lo), (b_hi, b_lo) = a, b
    dot = functools.partial(
        lax.dot_general, dimension_numbers=dims, preferred_element_type=jnp.float32
    )
    return dot(a_hi, b_hi) + (dot(a_hi, b_lo) + dot(a_lo, b_hi))


def span(start, size, unit=8):
    return pl.ds(pl.multiple_of(start, unit), size)


def window_kernel(
    x_ref, f_ref, d_ref, p_ref, fp_ref, c_ref, nd_ref,
    gram_ref, part_ref, w_ref, mhi_ref, mlo_ref, chi_ref, clo_ref, whi_ref, wlo_ref,
    xb_ref, fhi_ref, flo_ref, fphi_ref, fplo_ref, sq_ref, sqp_ref, sqrow_ref, spare_ref,
):
    K = 2 * HALF
    width = x_ref.shape[1]
    n_piv = p_ref.shape[0]
    blocks = n_piv // K
    fhi_ref[...], flo_ref[...] = halves(f_ref[...])
    wide = x_ref[...].astype(jnp.float32)
    sq_ref[...] = jnp.sum(wide * wide, axis=1, keepdims=True)
    ones = jnp.ones((8, width), jnp.bfloat16)
    eye = lax.broadcasted_iota(jnp.int32, (K, K), 0) == lax.broadcasted_iota(jnp.int32, (K, K), 1)

    def residual(rows, sq, f, points, sq_row, fp):
        inner = lax.dot_general(rows, points, NT, preferred_element_type=jnp.float32)
        return jnp.exp(2.0 * inner - sq - sq_row) - dot_split(f, fp, NT)

    def factor_half(start):
        rows = [w_ref[pl.ds(start + 8 * i, 8), start : start + HALF] for i in range(HALF // 8)]
        for i, row in enumerate(inverse_factor(rows, spare_ref)):
            w_ref[pl.ds(start + 8 * i, 8), start : start + HALF] = row

    def block(b, total):
        at = span(b * K, K, K)
        points = p_ref[at, :]
        xb_ref[at, :] = points.astype(jnp.bfloat16)
        fphi_ref[at, :], fplo_ref[at, :] = halves(fp_ref[at, :])
        squares = points * points
        sqp_ref[...] = jnp.sum(squares, axis=1, keepdims=True)
        sq_hi, sq_lo = halves(squares)
        sq_row = lax.dot_general(ones, sq_hi, NT, preferred_element_type=jnp.float32)
        sq_row = sq_row + lax.dot_general(ones, sq_lo, NT, preferred_element_type=jnp.float32)
        sqrow_ref[span(8 * b, 8), :] = sq_row
        sq_row = sq_row[0:1, :]
        fp = (fphi_ref[at, :], fplo_ref[at, :])
        gram_ref[...] = residual(xb_ref[at, :], sqp_ref[...], fp, xb_ref[at, :], sq_row, fp)

        def earlier(c, _):
            to = span(c * K, K, K)
            part_ref[...] = residual(
                xb_ref[at, :], sqp_ref[...], (fphi_ref[at, :], fplo_ref[at, :]),
                xb_ref[to, :], sqrow_ref[span(8 * c, 8), :][0:1, :], (fphi_ref[to, :], fplo_ref[to, :]),
            )

            def before(e, _):
                by = span(e * K, K, K)
                part_ref[...] = part_ref[...] - dot_split(
                    (mhi_ref[at, by], mlo_ref[at, by]), (mhi_ref[to, by], mlo_ref[to, by]), NT
                )
                return 0

            lax.fori_loop(0, c, before, 0)
            m = halves(dot_split(halves(part_ref[...]), (whi_ref[to, :], wlo_ref[to, :]), NT))
            mhi_ref[at, to], mlo_ref[at, to] = m
            gram_ref[...] = gram_ref[...] - dot_split(m, m, NT)
            return 0

        lax.fori_loop(0, b, earlier, 0)
        gram = gram_ref[...]
        diag = jnp.sum(jnp.where(eye, gram, 0.0), axis=0, keepdims=True)
        off = jnp.sum(jnp.abs(gram), axis=0, keepdims=True) - jnp.abs(diag)
        shift = ridge_base + jnp.maximum(jnp.max(off - diag, axis=1, keepdims=True), 0.0)
        w_ref[...] = gram + jnp.where(eye, shift, 0.0)

        c_ref[0:256, at] = residual(
            x_ref[0:256, :], sq_ref[0:256, :], (fhi_ref[0:256, :], flo_ref[0:256, :]), xb_ref[at, :], sq_row,
            (fphi_ref[at, :], fplo_ref[at, :]),
        )
        factor_half(0)
        first = w_ref[:HALF, :HALF]
        low = dot_exact(w_ref[HALF:, :HALF], first, NT)
        w_ref[HALF:, HALF:] = w_ref[HALF:, HALF:] - dot_exact(low, low, NT)
        carried = dot_exact(low, first, NN)
        c_ref[256:512, at] = residual(
            x_ref[256:512, :], sq_ref[256:512, :], (fhi_ref[256:512, :], flo_ref[256:512, :]), xb_ref[at, :], sq_row,
            (fphi_ref[at, :], fplo_ref[at, :]),
        )
        factor_half(HALF)
        w_ref[HALF:, :HALF] = -dot_exact(w_ref[HALF:, HALF:], carried, NN)
        w_ref[:HALF, HALF:] = jnp.zeros((HALF, HALF), jnp.float32)
        inverse = halves(w_ref[...])
        whi_ref[at, :], wlo_ref[at, :] = inverse


        def carry(e, _):
            by = span(e * K, K, K)
            c_ref[:, at] = c_ref[:, at] - dot_split(
                (chi_ref[:, by], clo_ref[:, by]), (mhi_ref[at, by], mlo_ref[at, by]), NT
            )
            return 0

        lax.fori_loop(0, b, carry, 0)
        cols = dot_split(halves(c_ref[:, at]), (whi_ref[at, :], wlo_ref[at, :]), NT)
        c_ref[:, at] = cols
        chi_ref[:, at], clo_ref[:, at] = halves(cols)
        squared = cols * cols
        return total + squared[:, :HALF] + squared[:, HALF:]

    total = lax.fori_loop(0, blocks, block, jnp.zeros((x_ref.shape[0], HALF), jnp.float32))
    sums = dot_exact(jnp.ones((8, HALF), jnp.float32), total, NT)
    nd_ref[...] = d_ref[...] - sums[0:1, :]


def window(x, f, diag, points, factor_rows):
    rows, width = x.shape
    rank = f.shape[1]
    n_piv = points.shape[0]
    K = 2 * HALF
    half, single = jnp.bfloat16, jnp.float32
    cols, new_diag = pl.pallas_call(
        window_kernel,
        out_shape=(
            jax.ShapeDtypeStruct((rows, n_piv), single),
            jax.ShapeDtypeStruct((1, rows), single),
        ),
        in_specs=[pl.BlockSpec(memory_space=pltpu.VMEM)] * 5,
        out_specs=[pl.BlockSpec(memory_space=pltpu.VMEM)] * 2,
        scratch_shapes=[
            pltpu.VMEM((K, K), single),
            pltpu.VMEM((K, K), single),
            pltpu.VMEM((K, K), single),
            pltpu.VMEM((n_piv, n_piv), half),
            pltpu.VMEM((n_piv, n_piv), half),
            pltpu.VMEM((rows, n_piv), half),
            pltpu.VMEM((rows, n_piv), half),
            pltpu.VMEM((n_piv, K), half),
            pltpu.VMEM((n_piv, K), half),
            pltpu.VMEM((n_piv, width), half),
            pltpu.VMEM((rows, rank), half),
            pltpu.VMEM((rows, rank), half),
            pltpu.VMEM((n_piv, rank), half),
            pltpu.VMEM((n_piv, rank), half),
            pltpu.VMEM((rows, 1), single),
            pltpu.VMEM((K, 1), single),
            pltpu.VMEM((8 * (n_piv // K), K), single),
            pltpu.VMEM((144, HALF), single),
        ],
        compiler_params=pltpu.CompilerParams(vmem_limit_bytes=56 << 20),
        name="window",
    )(x, f, diag.reshape(1, rows), points, factor_rows)
    return cols, new_diag.reshape(rows)


MESH = pl.DeviceIdType.MESH
X, Y, Z = 4, 4, 8
PICK = 256


COPIES = 4 + 6 + 6 + 7 + 7 + 6 + 6 + 5


def gather_kernel(*refs):
    n_lanes = 2
    row_ref, x_ref, f_ref = refs[:3]
    third_ref, send, recv = refs[-3:]
    refs = refs[3:-3]
    outs, picked, scratch = refs[:n_lanes], refs[n_lanes : 2 * n_lanes], refs[2 * n_lanes :]
    where = lax.axis_index("rows")
    x = lax.axis_index("sub")
    core = where % 2
    y = (where // 2) % Y
    z = where // (2 * Y)
    p1 = x * (1 - core) + y * core
    p2 = y * (1 - core) + x * core

    def device(q1, q2, qz):
        qx = q1 * (1 - core) + q2 * core
        qy = q2 * (1 - core) + q1 * core
        return ((qz * Y + qy) * 2 + core, qx)

    sibling = ((z * Y + y) * 2 + 1 - core, x)
    right1, left1 = device((p1 + 1) % X, p2, z), device((p1 + 3) % X, p2, z)
    right2, left2 = device(p1, (p2 + 1) % Y, z), device(p1, (p2 + 3) % Y, z)
    along_z = [device(p1, p2, (z + d) % Z) for d in range(1, Z)]

    barrier = pltpu.get_barrier_semaphore()
    partners = [sibling, right1, left1, right2, left2] + along_z
    for partner in partners:
        pl.semaphore_signal(barrier, inc=1, device_id=partner, device_id_type=MESH)

    rest = f_ref[...]
    for k in range(3):
        third_ref[k] = rest.astype(jnp.bfloat16)
        rest = rest - third_ref[k].astype(jnp.float32)
    local_rows = x_ref.shape[0]

    def pick(b, _):
        at = pl.ds(pl.multiple_of(b * PICK, PICK), PICK)
        places = lax.broadcasted_iota(jnp.int32, (PICK, local_rows), 1)
        chosen = jnp.where(row_ref[at, :] == places, 1.0, 0.0).astype(jnp.bfloat16)
        dot = functools.partial(jnp.dot, chosen, preferred_element_type=jnp.float32)
        picked[0][at, :] = dot(x_ref[...])
        picked[1][at, :] = (dot(third_ref[0]) + dot(third_ref[1])) + dot(third_ref[2])
        return 0

    lax.fori_loop(0, row_ref.shape[0] // PICK, pick, 0)
    pl.semaphore_wait(barrier, len(partners))

    started = []

    def copy(src, dst, target):
        k = len(started)
        made = pltpu.make_async_remote_copy(
            src_ref=src, dst_ref=dst, send_sem=send.at[k], recv_sem=recv.at[k],
            device_id=target, device_id_type=MESH,
        )
        made.start()
        started.append(made)
        return made

    def span(start, size):
        return pl.ds(pl.multiple_of(start, 8), size)

    def travel(s_ref, out_ref, sib, near1, near2, near3):
        n_piv, width = s_ref.shape
        half = n_piv // 2
        piece1, piece2, piece3 = half // X, half // X // Y, 8
        cut = width // 2

        order = (2, 1, 3, 0)
        from_sibling = {}
        for d in order:
            q = (p2 + d) % X
            from_sibling[d] = copy(
                s_ref.at[span((1 - core) * half + q * piece1, piece1), :],
                sib.at[span(q * piece1, piece1), :],
                sibling,
            )
        yield

        def merge(d):
            q = (p1 + d) % X
            from_sibling[d].wait_recv()
            at = span(q * piece1, piece1)
            sib[at, :] = sib[at, :] + s_ref[span(core * half + q * piece1, piece1), :]

        def scatter(base, piece, p, right, left, near, ready):
            hp = piece // 2

            def rows(d, part):
                return span(base + ((p + d) % 4) * piece + part * hp, hp)

            ready(2)
            over_right = copy(sib.at[rows(2, 0), :], near.at[0], right)
            over_left = copy(sib.at[rows(2, 1), :], near.at[1], left)
            ready(1)
            plain_right = copy(sib.at[rows(1, 1), :], near.at[2], right)
            ready(3)
            plain_left = copy(sib.at[rows(3, 0), :], near.at[3], left)
            ready(0)
            yield
            over_right.wait_recv()
            sib[rows(1, 0), :] = sib[rows(1, 0), :] + near[0]
            last_right = copy(sib.at[rows(1, 0), :], near.at[4], right)
            over_left.wait_recv()
            sib[rows(3, 1), :] = sib[rows(3, 1), :] + near[1]
            last_left = copy(sib.at[rows(3, 1), :], near.at[5], left)
            yield
            plain_right.wait_recv()
            sib[rows(0, 1), :] = sib[rows(0, 1), :] + near[2]
            plain_left.wait_recv()
            sib[rows(0, 0), :] = sib[rows(0, 0), :] + near[3]
            last_right.wait_recv()
            sib[rows(0, 0), :] = sib[rows(0, 0), :] + near[4]
            last_left.wait_recv()
            sib[rows(0, 1), :] = sib[rows(0, 1), :] + near[5]

        yield from scatter(0, piece1, p1, right1, left1, near1, merge)
        base2 = p1 * piece1
        yield from scatter(base2, piece2, p2, right2, left2, near2, lambda d: None)
        base3 = base2 + p2 * piece2

        def cell(base, q):
            return span(base + (q // 2) * piece3, piece3), pl.ds(
                pl.multiple_of((q % 2) * cut, 128), cut
            )

        arriving = []
        for d in range(1, Z):
            arriving.append(
                copy(sib.at[cell(base3, (z + d) % Z)], near3.at[d - 1], along_z[d - 1])
            )
        yield
        total = sib[cell(base3, z)]
        for d in range(1, Z):
            arriving[d - 1].wait_recv()
            total = total + near3[d - 1]
        mine = cell(core * half + base3, z)
        out_ref[mine] = total
        arriving = [
            copy(out_ref.at[mine], out_ref.at[mine], along_z[d - 1]) for d in range(1, Z)
        ]
        yield
        for made in arriving:
            made.wait_recv()

        def gather(base, piece, p, right, left, done):
            hp = piece // 2

            def rows(d, part, size):
                return span(base + ((p + d) % 4) * piece + part * hp, size)

            parts = [out_ref.at[rows(0, k, hp), :] for k in range(2)]
            from_left = [copy(parts[0], parts[0], right)]
            from_right = [copy(parts[1], parts[1], left)]
            from_left += [copy(parts[1], parts[1], right)]
            from_right += [copy(parts[0], parts[0], left)]
            done(rows(0, 0, piece))
            yield
            from_left[0].wait_recv()
            on = out_ref.at[rows(3, 0, hp), :]
            far_left = copy(on, on, right)
            from_right[0].wait_recv()
            on = out_ref.at[rows(1, 1, hp), :]
            far_right = copy(on, on, left)
            from_left[1].wait_recv()
            done(rows(3, 0, piece))
            from_right[1].wait_recv()
            done(rows(1, 0, piece))
            yield
            far_left.wait_recv()
            done(rows(2, 0, hp))
            far_right.wait_recv()
            done(rows(2, 1, hp))

        yield from gather(core * half + base2, piece2, p2, right2, left2, lambda at: None)
        across = []

        def hand_over(at):
            across.append(copy(out_ref.at[at, :], out_ref.at[at, :], sibling))

        yield from gather(core * half, piece1, p1, right1, left1, hand_over)
        yield
        for made in across:
            made.wait_recv()

    ways = [
        travel(picked[i], outs[i], *scratch[4 * i : 4 * i + 4]) for i in range(n_lanes)
    ]
    while ways:
        ways = [way for way in ways if next(way, True) is None]
    for made in started:
        made.wait_send()


def gather_rows(row, x, f):
    n_piv = row.shape[0]
    half = n_piv // 2
    widths = (x.shape[1], f.shape[1])
    scratch = [pltpu.VMEM((n_piv, width), jnp.float32) for width in widths]
    for width in widths:
        scratch += [
            pltpu.VMEM((half, width), jnp.float32),
            pltpu.VMEM((6, half // X // 2, width), jnp.float32),
            pltpu.VMEM((6, half // X // Y // 2, width), jnp.float32),
            pltpu.VMEM((Z - 1, 8, width // 2), jnp.float32),
        ]
    scratch += [pltpu.VMEM((3,) + f.shape, jnp.bfloat16)]
    copies = COPIES * len(widths)
    return pl.pallas_call(
        gather_kernel,
        out_shape=tuple(jax.ShapeDtypeStruct((n_piv, width), jnp.float32) for width in widths),
        in_specs=[pl.BlockSpec(memory_space=pltpu.VMEM)] * 3,
        out_specs=[pl.BlockSpec(memory_space=pltpu.VMEM)] * 2,
        scratch_shapes=scratch
        + [pltpu.SemaphoreType.DMA((copies,)), pltpu.SemaphoreType.DMA((copies,))],
        compiler_params=pltpu.CompilerParams(
            collective_id=0, has_side_effects=True, vmem_limit_bytes=40 << 20
        ),
        name="gather_rows",
    )(row, x, f)


def on_device(embeddings, factor, diagonal, pivot_owner, pivot_local):
    device = lax.axis_index("rows") * lax.axis_size("sub") + lax.axis_index("sub")
    row = jnp.where(pivot_owner == device, pivot_local, -1).reshape(-1, 1)
    points, factor_rows = gather_rows(row, embeddings, factor)
    return window(embeddings, factor, diagonal, points, factor_rows)


def solution(mesh):
    return jax.shard_map(
        on_device,
        mesh=mesh,
        in_specs=(P(("rows", "sub"), None), P(("rows", "sub"), None), P(("rows", "sub")), P(), P()),
        out_specs=(P(("rows", "sub"), None), P(("rows", "sub"))),
        check_vma=False,
    )
```

```python
import functools
import jax
import jax.numpy as jnp
from jax import lax
from jax.experimental import pallas as pl
from jax.experimental.pallas import tpu as pltpu
from jax.sharding import PartitionSpec as P

ridge_base = 0.5
HALF = 128
NT = (((1,), (1,)), ((), ()))
NN = (((1,), (0,)), ((), ()))


def lane_splat(a, c):
    return jnp.broadcast_to(a[:, c : c + 1], (8, HALF))


def inverse_factor(rows, spare):
    sub = lax.broadcasted_iota(jnp.int32, (8, HALF), 0)
    lane = lax.broadcasted_iota(jnp.int32, (8, HALF), 1)
    rows = list(rows)
    groups = len(rows)
    near = 2
    out = []
    for g in range(groups):
        base = 8 * g

        def splats(value, slot, which):
            start = (g % 2) * 72 + 8 * slot
            spare[start : start + 8, :] = value
            return [jnp.broadcast_to(spare[start + k : start + k + 1, :], (8, HALF)) for k in which]

        inside = (lane >= base) & (lane < base + 8)
        start = jnp.where(inside, jnp.where(lane == sub + base, 1.0, 0.0), rows[g])
        a = [splats(lane_splat(rows[g], base + c), c, range(c + 1)) for c in range(8)]
        y = splats(start, 8, range(8))
        inverses, factors, pivots, forward = [], [], [], []
        for j in range(0, 8, 2):
            p, q, r = a[j][j], a[j + 1][j], a[j + 1][j + 1]
            det = p * r - q * q
            recip = 1.0 / det
            first = 1.0 / p
            pivots += [p, det * first]
            forward += [y[j], y[j + 1] - (q * first) * y[j]]
            inverses.append((r * recip, q * recip, p * recip))
            factor = {
                c: ((a[c][j] * r - a[c][j + 1] * q) * recip, (a[c][j + 1] * p - a[c][j] * q) * recip)
                for c in range(j + 2, 8)
            }
            factors.append(factor)
            for k in range(j + 2, 8):
                for c in range(k, 8):
                    a[c][k] = a[c][k] - (factor[k][0] * a[c][j] + factor[k][1] * a[c][j + 1])
                y[k] = y[k] - (factor[k][0] * y[j] + factor[k][1] * y[j + 1])
        done, scale = forward[0], pivots[0]
        for k in range(1, 8):
            done = jnp.where(sub == k, forward[k], done)
            scale = jnp.where(sub == k, pivots[k], scale)
        out.append(jnp.where(lane < base + 8, done * lax.rsqrt(scale), 0.0))
        solved = [None] * 8
        for j in (6, 4, 2, 0):
            left, cross, right = inverses[j // 2]
            top = left * y[j] - cross * y[j + 1]
            bottom = right * y[j + 1] - cross * y[j]
            for k in range(7, j + 1, -1):
                top = top - factors[j // 2][k][0] * solved[k]
                bottom = bottom - factors[j // 2][k][1] * solved[k]
            solved[j], solved[j + 1] = top, bottom
        for i in range(g + 1, min(groups, g + 1 + near)):
            t = [lane_splat(rows[i], base + k) * solved[k] for k in range(8)]
            total = ((t[0] + t[1]) + (t[2] + t[3])) + ((t[4] + t[5]) + (t[6] + t[7]))
            rows[i] = jnp.where(inside, 0.0, rows[i]) - total
        if g + 1 + near < groups:
            merged = solved[0]
            for k in range(1, 8):
                merged = jnp.where(sub == k, solved[k], merged)
            zero = jnp.zeros((8, HALF), jnp.float32)
            weights = jnp.concatenate([merged if k == g else zero for k in range(groups)], axis=0)
            change = dot_exact(jnp.concatenate(rows[g + 1 + near :], axis=0), weights, NN)
            for k, i in enumerate(range(g + 1 + near, groups)):
                rows[i] = jnp.where(inside, 0.0, rows[i]) - change[8 * k : 8 * k + 8]
    return out


def dot_exact(a, b, dims):
    return lax.dot_general(
        a, b, dims, precision=lax.Precision.HIGHEST, preferred_element_type=jnp.float32
    )


def halves(a):
    high = a.astype(jnp.bfloat16)
    return high, (a - high.astype(jnp.float32)).astype(jnp.bfloat16)


def dot_split(a, b, dims):
    (a_hi, a_lo), (b_hi, b_lo) = a, b
    dot = functools.partial(
        lax.dot_general, dimension_numbers=dims, preferred_element_type=jnp.float32
    )
    return dot(a_hi, b_hi) + (dot(a_hi, b_lo) + dot(a_lo, b_hi))


def span(start, size, unit=8):
    return pl.ds(pl.multiple_of(start, unit), size)


def window_kernel(
    x_ref, f_ref, d_ref, p_ref, fp_ref, c_ref, nd_ref,
    gram_ref, part_ref, w_ref, mhi_ref, mlo_ref, chi_ref, clo_ref, whi_ref, wlo_ref,
    xb_ref, fhi_ref, flo_ref, fphi_ref, fplo_ref, sq_ref, sqp_ref, sqrow_ref, spare_ref,
):
    K = 2 * HALF
    width = x_ref.shape[1]
    n_piv = p_ref.shape[0]
    blocks = n_piv // K
    fhi_ref[...], flo_ref[...] = halves(f_ref[...])
    wide = x_ref[...].astype(jnp.float32)
    sq_ref[...] = jnp.sum(wide * wide, axis=1, keepdims=True)
    ones = jnp.ones((8, width), jnp.bfloat16)
    eye = lax.broadcasted_iota(jnp.int32, (K, K), 0) == lax.broadcasted_iota(jnp.int32, (K, K), 1)

    def residual(rows, sq, f, points, sq_row, fp):
        inner = lax.dot_general(rows, points, NT, preferred_element_type=jnp.float32)
        return jnp.exp(2.0 * inner - sq - sq_row) - dot_split(f, fp, NT)

    def factor_half(start):
        rows = [w_ref[pl.ds(start + 8 * i, 8), start : start + HALF] for i in range(HALF // 8)]
        for i, row in enumerate(inverse_factor(rows, spare_ref)):
            w_ref[pl.ds(start + 8 * i, 8), start : start + HALF] = row

    def block(b, total):
        at = span(b * K, K, K)
        points = p_ref[at, :]
        xb_ref[at, :] = points.astype(jnp.bfloat16)
        fphi_ref[at, :], fplo_ref[at, :] = halves(fp_ref[at, :])
        squares = points * points
        sqp_ref[...] = jnp.sum(squares, axis=1, keepdims=True)
        sq_hi, sq_lo = halves(squares)
        sq_row = lax.dot_general(ones, sq_hi, NT, preferred_element_type=jnp.float32)
        sq_row = sq_row + lax.dot_general(ones, sq_lo, NT, preferred_element_type=jnp.float32)
        sqrow_ref[span(8 * b, 8), :] = sq_row
        sq_row = sq_row[0:1, :]
        fp = (fphi_ref[at, :], fplo_ref[at, :])
        gram_ref[...] = residual(xb_ref[at, :], sqp_ref[...], fp, xb_ref[at, :], sq_row, fp)

        def earlier(c, _):
            to = span(c * K, K, K)
            part_ref[...] = residual(
                xb_ref[at, :], sqp_ref[...], (fphi_ref[at, :], fplo_ref[at, :]),
                xb_ref[to, :], sqrow_ref[span(8 * c, 8), :][0:1, :], (fphi_ref[to, :], fplo_ref[to, :]),
            )

            def before(e, _):
                by = span(e * K, K, K)
                part_ref[...] = part_ref[...] - dot_split(
                    (mhi_ref[at, by], mlo_ref[at, by]), (mhi_ref[to, by], mlo_ref[to, by]), NT
                )
                return 0

            lax.fori_loop(0, c, before, 0)
            m = halves(dot_split(halves(part_ref[...]), (whi_ref[to, :], wlo_ref[to, :]), NT))
            mhi_ref[at, to], mlo_ref[at, to] = m
            gram_ref[...] = gram_ref[...] - dot_split(m, m, NT)
            return 0

        lax.fori_loop(0, b, earlier, 0)
        gram = gram_ref[...]
        diag = jnp.sum(jnp.where(eye, gram, 0.0), axis=0, keepdims=True)
        off = jnp.sum(jnp.abs(gram), axis=0, keepdims=True) - jnp.abs(diag)
        shift = ridge_base + jnp.maximum(jnp.max(off - diag, axis=1, keepdims=True), 0.0)
        w_ref[...] = gram + jnp.where(eye, shift, 0.0)

        c_ref[0:256, at] = residual(
            x_ref[0:256, :], sq_ref[0:256, :], (fhi_ref[0:256, :], flo_ref[0:256, :]), xb_ref[at, :], sq_row,
            (fphi_ref[at, :], fplo_ref[at, :]),
        )
        factor_half(0)
        first = w_ref[:HALF, :HALF]
        low = dot_exact(w_ref[HALF:, :HALF], first, NT)
        w_ref[HALF:, HALF:] = w_ref[HALF:, HALF:] - dot_exact(low, low, NT)
        carried = dot_exact(low, first, NN)
        c_ref[256:512, at] = residual(
            x_ref[256:512, :], sq_ref[256:512, :], (fhi_ref[256:512, :], flo_ref[256:512, :]), xb_ref[at, :], sq_row,
            (fphi_ref[at, :], fplo_ref[at, :]),
        )
        factor_half(HALF)
        w_ref[HALF:, :HALF] = -dot_exact(w_ref[HALF:, HALF:], carried, NN)
        w_ref[:HALF, HALF:] = jnp.zeros((HALF, HALF), jnp.float32)
        inverse = halves(w_ref[...])
        whi_ref[at, :], wlo_ref[at, :] = inverse


        def carry(e, _):
            by = span(e * K, K, K)
            c_ref[:, at] = c_ref[:, at] - dot_split(
                (chi_ref[:, by], clo_ref[:, by]), (mhi_ref[at, by], mlo_ref[at, by]), NT
            )
            return 0

        lax.fori_loop(0, b, carry, 0)
        cols = dot_split(halves(c_ref[:, at]), (whi_ref[at, :], wlo_ref[at, :]), NT)
        c_ref[:, at] = cols
        chi_ref[:, at], clo_ref[:, at] = halves(cols)
        squared = cols * cols
        return total + squared[:, :HALF] + squared[:, HALF:]

    total = lax.fori_loop(0, blocks, block, jnp.zeros((x_ref.shape[0], HALF), jnp.float32))
    sums = dot_exact(jnp.ones((8, HALF), jnp.float32), total, NT)
    nd_ref[...] = d_ref[...] - sums[0:1, :]


def window(x, f, diag, points, factor_rows):
    rows, width = x.shape
    rank = f.shape[1]
    n_piv = points.shape[0]
    K = 2 * HALF
    half, single = jnp.bfloat16, jnp.float32
    cols, new_diag = pl.pallas_call(
        window_kernel,
        out_shape=(
            jax.ShapeDtypeStruct((rows, n_piv), single),
            jax.ShapeDtypeStruct((1, rows), single),
        ),
        in_specs=[pl.BlockSpec(memory_space=pltpu.VMEM)] * 5,
        out_specs=[pl.BlockSpec(memory_space=pltpu.VMEM)] * 2,
        scratch_shapes=[
            pltpu.VMEM((K, K), single),
            pltpu.VMEM((K, K), single),
            pltpu.VMEM((K, K), single),
            pltpu.VMEM((n_piv, n_piv), half),
            pltpu.VMEM((n_piv, n_piv), half),
            pltpu.VMEM((rows, n_piv), half),
            pltpu.VMEM((rows, n_piv), half),
            pltpu.VMEM((n_piv, K), half),
            pltpu.VMEM((n_piv, K), half),
            pltpu.VMEM((n_piv, width), half),
            pltpu.VMEM((rows, rank), half),
            pltpu.VMEM((rows, rank), half),
            pltpu.VMEM((n_piv, rank), half),
            pltpu.VMEM((n_piv, rank), half),
            pltpu.VMEM((rows, 1), single),
            pltpu.VMEM((K, 1), single),
            pltpu.VMEM((8 * (n_piv // K), K), single),
            pltpu.VMEM((144, HALF), single),
        ],
        compiler_params=pltpu.CompilerParams(vmem_limit_bytes=30 << 20),
        name="window",
    )(x, f, diag.reshape(1, rows), points, factor_rows)
    return cols, new_diag.reshape(rows)


MESH = pl.DeviceIdType.MESH
X, Y, Z = 4, 4, 8
PICK = 256


COPIES = 4 + 6 + 6 + 7 + 7 + 6 + 6 + 5


def gather_kernel(*refs):
    n_lanes = 2
    row_ref, x_ref, f_ref = refs[:3]
    third_ref, send, recv = refs[-3:]
    refs = refs[3:-3]
    outs, picked, scratch = refs[:n_lanes], refs[n_lanes : 2 * n_lanes], refs[2 * n_lanes :]
    where = lax.axis_index("rows")
    x = lax.axis_index("sub")
    core = where % 2
    y = (where // 2) % Y
    z = where // (2 * Y)
    p1 = x * (1 - core) + y * core
    p2 = y * (1 - core) + x * core

    def device(q1, q2, qz):
        qx = q1 * (1 - core) + q2 * core
        qy = q2 * (1 - core) + q1 * core
        return ((qz * Y + qy) * 2 + core, qx)

    sibling = ((z * Y + y) * 2 + 1 - core, x)
    right1, left1 = device((p1 + 1) % X, p2, z), device((p1 + 3) % X, p2, z)
    right2, left2 = device(p1, (p2 + 1) % Y, z), device(p1, (p2 + 3) % Y, z)
    along_z = [device(p1, p2, (z + d) % Z) for d in range(1, Z)]

    barrier = pltpu.get_barrier_semaphore()
    partners = [sibling, right1, left1, right2, left2] + along_z
    for partner in partners:
        pl.semaphore_signal(barrier, inc=1, device_id=partner, device_id_type=MESH)

    rest = f_ref[...]
    for k in range(3):
        third_ref[k] = rest.astype(jnp.bfloat16)
        rest = rest - third_ref[k].astype(jnp.float32)
    local_rows = x_ref.shape[0]

    def pick(b, _):
        at = pl.ds(pl.multiple_of(b * PICK, PICK), PICK)
        places = lax.broadcasted_iota(jnp.int32, (PICK, local_rows), 1)
        chosen = jnp.where(row_ref[at, :] == places, 1.0, 0.0).astype(jnp.bfloat16)
        dot = functools.partial(jnp.dot, chosen, preferred_element_type=jnp.float32)
        picked[0][at, :] = dot(x_ref[...])
        picked[1][at, :] = (dot(third_ref[0]) + dot(third_ref[1])) + dot(third_ref[2])
        return 0

    lax.fori_loop(0, row_ref.shape[0] // PICK, pick, 0)
    pl.semaphore_wait(barrier, len(partners))

    started = []

    def copy(src, dst, target):
        k = len(started)
        made = pltpu.make_async_remote_copy(
            src_ref=src, dst_ref=dst, send_sem=send.at[k], recv_sem=recv.at[k],
            device_id=target, device_id_type=MESH,
        )
        made.start()
        started.append(made)
        return made

    def span(start, size):
        return pl.ds(pl.multiple_of(start, 8), size)

    def travel(s_ref, out_ref, sib, near1, near2, near3):
        n_piv, width = s_ref.shape
        half = n_piv // 2
        piece1, piece2, piece3 = half // X, half // X // Y, 8
        cut = width // 2

        order = (2, 1, 3, 0)
        from_sibling = {}
        for d in order:
            q = (p2 + d) % X
            from_sibling[d] = copy(
                s_ref.at[span((1 - core) * half + q * piece1, piece1), :],
                sib.at[span(q * piece1, piece1), :],
                sibling,
            )
        yield

        def merge(d):
            q = (p1 + d) % X
            from_sibling[d].wait_recv()
            at = span(q * piece1, piece1)
            sib[at, :] = sib[at, :] + s_ref[span(core * half + q * piece1, piece1), :]

        def scatter(base, piece, p, right, left, near, ready):
            hp = piece // 2

            def rows(d, part):
                return span(base + ((p + d) % 4) * piece + part * hp, hp)

            ready(2)
            over_right = copy(sib.at[rows(2, 0), :], near.at[0], right)
            over_left = copy(sib.at[rows(2, 1), :], near.at[1], left)
            ready(1)
            plain_right = copy(sib.at[rows(1, 1), :], near.at[2], right)
            ready(3)
            plain_left = copy(sib.at[rows(3, 0), :], near.at[3], left)
            ready(0)
            yield
            over_right.wait_recv()
            sib[rows(1, 0), :] = sib[rows(1, 0), :] + near[0]
            last_right = copy(sib.at[rows(1, 0), :], near.at[4], right)
            over_left.wait_recv()
            sib[rows(3, 1), :] = sib[rows(3, 1), :] + near[1]
            last_left = copy(sib.at[rows(3, 1), :], near.at[5], left)
            yield
            plain_right.wait_recv()
            sib[rows(0, 1), :] = sib[rows(0, 1), :] + near[2]
            plain_left.wait_recv()
            sib[rows(0, 0), :] = sib[rows(0, 0), :] + near[3]
            last_right.wait_recv()
            sib[rows(0, 0), :] = sib[rows(0, 0), :] + near[4]
            last_left.wait_recv()
            sib[rows(0, 1), :] = sib[rows(0, 1), :] + near[5]

        yield from scatter(0, piece1, p1, right1, left1, near1, merge)
        base2 = p1 * piece1
        yield from scatter(base2, piece2, p2, right2, left2, near2, lambda d: None)
        base3 = base2 + p2 * piece2

        def cell(base, q):
            return span(base + (q // 2) * piece3, piece3), pl.ds(
                pl.multiple_of((q % 2) * cut, 128), cut
            )

        arriving = []
        for d in range(1, Z):
            arriving.append(
                copy(sib.at[cell(base3, (z + d) % Z)], near3.at[d - 1], along_z[d - 1])
            )
        yield
        total = sib[cell(base3, z)]
        for d in range(1, Z):
            arriving[d - 1].wait_recv()
            total = total + near3[d - 1]
        mine = cell(core * half + base3, z)
        out_ref[mine] = total
        arriving = [
            copy(out_ref.at[mine], out_ref.at[mine], along_z[d - 1]) for d in range(1, Z)
        ]
        yield
        for made in arriving:
            made.wait_recv()

        def gather(base, piece, p, right, left, done):
            hp = piece // 2

            def rows(d, part, size):
                return span(base + ((p + d) % 4) * piece + part * hp, size)

            parts = [out_ref.at[rows(0, k, hp), :] for k in range(2)]
            from_left = [copy(parts[0], parts[0], right)]
            from_right = [copy(parts[1], parts[1], left)]
            from_left += [copy(parts[1], parts[1], right)]
            from_right += [copy(parts[0], parts[0], left)]
            done(rows(0, 0, piece))
            yield
            from_left[0].wait_recv()
            on = out_ref.at[rows(3, 0, hp), :]
            far_left = copy(on, on, right)
            from_right[0].wait_recv()
            on = out_ref.at[rows(1, 1, hp), :]
            far_right = copy(on, on, left)
            from_left[1].wait_recv()
            done(rows(3, 0, piece))
            from_right[1].wait_recv()
            done(rows(1, 0, piece))
            yield
            far_left.wait_recv()
            done(rows(2, 0, hp))
            far_right.wait_recv()
            done(rows(2, 1, hp))

        yield from gather(core * half + base2, piece2, p2, right2, left2, lambda at: None)
        across = []

        def hand_over(at):
            across.append(copy(out_ref.at[at, :], out_ref.at[at, :], sibling))

        yield from gather(core * half, piece1, p1, right1, left1, hand_over)
        yield
        for made in across:
            made.wait_recv()

    ways = [
        travel(picked[i], outs[i], *scratch[4 * i : 4 * i + 4]) for i in range(n_lanes)
    ]
    while ways:
        ways = [way for way in ways if next(way, True) is None]
    for made in started:
        made.wait_send()


def gather_rows(row, x, f):
    n_piv = row.shape[0]
    half = n_piv // 2
    widths = (x.shape[1], f.shape[1])
    scratch = [pltpu.VMEM((n_piv, width), jnp.float32) for width in widths]
    for width in widths:
        scratch += [
            pltpu.VMEM((half, width), jnp.float32),
            pltpu.VMEM((6, half // X // 2, width), jnp.float32),
            pltpu.VMEM((6, half // X // Y // 2, width), jnp.float32),
            pltpu.VMEM((Z - 1, 8, width // 2), jnp.float32),
        ]
    scratch += [pltpu.VMEM((3,) + f.shape, jnp.bfloat16)]
    copies = COPIES * len(widths)
    return pl.pallas_call(
        gather_kernel,
        out_shape=tuple(jax.ShapeDtypeStruct((n_piv, width), jnp.float32) for width in widths),
        in_specs=[pl.BlockSpec(memory_space=pltpu.VMEM)] * 3,
        out_specs=[pl.BlockSpec(memory_space=pltpu.VMEM)] * 2,
        scratch_shapes=scratch
        + [pltpu.SemaphoreType.DMA((copies,)), pltpu.SemaphoreType.DMA((copies,))],
        compiler_params=pltpu.CompilerParams(
            collective_id=0, has_side_effects=True, vmem_limit_bytes=40 << 20
        ),
        name="gather_rows",
    )(row, x, f)


def on_device(embeddings, factor, diagonal, pivot_owner, pivot_local):
    device = lax.axis_index("rows") * lax.axis_size("sub") + lax.axis_index("sub")
    row = jnp.where(pivot_owner == device, pivot_local, -1).reshape(-1, 1)
    points, factor_rows = gather_rows(row, embeddings, factor)
    return window(embeddings, factor, diagonal, points, factor_rows)


def solution(mesh):
    return jax.shard_map(
        on_device,
        mesh=mesh,
        in_specs=(P(("rows", "sub"), None), P(("rows", "sub"), None), P(("rows", "sub")), P(), P()),
        out_specs=(P(("rows", "sub"), None), P(("rows", "sub"))),
        check_vma=False,
    )
```

```python
import functools
import jax
import jax.numpy as jnp
from jax import lax
from jax.experimental import pallas as pl
from jax.experimental.pallas import tpu as pltpu
from jax.sharding import PartitionSpec as P

ridge_base = 0.5
HALF = 128
NT = (((1,), (1,)), ((), ()))
NN = (((1,), (0,)), ((), ()))


def lane_splat(a, c):
    return jnp.broadcast_to(a[:, c : c + 1], (8, HALF))


def inverse_factor(rows, spare):
    sub = lax.broadcasted_iota(jnp.int32, (8, HALF), 0)
    lane = lax.broadcasted_iota(jnp.int32, (8, HALF), 1)
    rows = list(rows)
    groups = len(rows)
    out = []
    for g in range(groups):
        base = 8 * g

        def splats(value, slot, which):
            start = (g % 2) * 72 + 8 * slot
            spare[start : start + 8, :] = value
            return [jnp.broadcast_to(spare[start + k : start + k + 1, :], (8, HALF)) for k in which]

        inside = (lane >= base) & (lane < base + 8)
        start = jnp.where(inside, jnp.where(lane == sub + base, 1.0, 0.0), rows[g])
        a = [splats(lane_splat(rows[g], base + c), c, range(c + 1)) for c in range(8)]
        y = splats(start, 8, range(8))
        inverses, factors, pivots, forward = [], [], [], []
        for j in range(0, 8, 2):
            p, q, r = a[j][j], a[j + 1][j], a[j + 1][j + 1]
            det = p * r - q * q
            recip = 1.0 / det
            first = 1.0 / p
            pivots += [p, det * first]
            forward += [y[j], y[j + 1] - (q * first) * y[j]]
            inverses.append((r * recip, q * recip, p * recip))
            factor = {
                c: ((a[c][j] * r - a[c][j + 1] * q) * recip, (a[c][j + 1] * p - a[c][j] * q) * recip)
                for c in range(j + 2, 8)
            }
            factors.append(factor)
            for k in range(j + 2, 8):
                for c in range(k, 8):
                    a[c][k] = a[c][k] - (factor[k][0] * a[c][j] + factor[k][1] * a[c][j + 1])
                y[k] = y[k] - (factor[k][0] * y[j] + factor[k][1] * y[j + 1])
        done, scale = forward[0], pivots[0]
        for k in range(1, 8):
            done = jnp.where(sub == k, forward[k], done)
            scale = jnp.where(sub == k, pivots[k], scale)
        out.append(jnp.where(lane < base + 8, done * lax.rsqrt(scale), 0.0))
        solved = [None] * 8
        for j in (6, 4, 2, 0):
            left, cross, right = inverses[j // 2]
            top = left * y[j] - cross * y[j + 1]
            bottom = right * y[j + 1] - cross * y[j]
            for k in range(7, j + 1, -1):
                top = top - factors[j // 2][k][0] * solved[k]
                bottom = bottom - factors[j // 2][k][1] * solved[k]
            solved[j], solved[j + 1] = top, bottom
        reach = 3 if g % 2 == 0 else 2
        for i in range(g + 1, min(groups, g + 1 + reach)):
            t = [lane_splat(rows[i], base + k) * solved[k] for k in range(8)]
            total = ((t[0] + t[1]) + (t[2] + t[3])) + ((t[4] + t[5]) + (t[6] + t[7]))
            rows[i] = jnp.where(inside, 0.0, rows[i]) - total
        merged = solved[0]
        for k in range(1, 8):
            merged = jnp.where(sub == k, solved[k], merged)
        if g % 2 == 0:
            before = merged
        elif g + 1 + reach < groups:
            t = [lane_splat(before, base + k) * solved[k] for k in range(8)]
            total = ((t[0] + t[1]) + (t[2] + t[3])) + ((t[4] + t[5]) + (t[6] + t[7]))
            pair = {g - 1: jnp.where(inside, 0.0, before) - total, g: merged}
            zero = jnp.zeros((8, HALF), jnp.float32)
            weights = jnp.concatenate([pair.get(k, zero) for k in range(groups)], axis=0)
            change = dot_exact(jnp.concatenate(rows[g + 1 + reach :], axis=0), weights, NN)
            both = (lane >= base - 8) & (lane < base + 8)
            for k, i in enumerate(range(g + 1 + reach, groups)):
                rows[i] = jnp.where(both, 0.0, rows[i]) - change[8 * k : 8 * k + 8]
    return out


def dot_exact(a, b, dims):
    return lax.dot_general(
        a, b, dims, precision=lax.Precision.HIGHEST, preferred_element_type=jnp.float32
    )


def halves(a):
    high = a.astype(jnp.bfloat16)
    return high, (a - high.astype(jnp.float32)).astype(jnp.bfloat16)


def dot_split(a, b, dims):
    (a_hi, a_lo), (b_hi, b_lo) = a, b
    dot = functools.partial(
        lax.dot_general, dimension_numbers=dims, preferred_element_type=jnp.float32
    )
    return dot(a_hi, b_hi) + (dot(a_hi, b_lo) + dot(a_lo, b_hi))


def span(start, size, unit=8):
    return pl.ds(pl.multiple_of(start, unit), size)


def window_kernel(
    x_ref, f_ref, d_ref, p_ref, fp_ref, c_ref, nd_ref,
    gram_ref, part_ref, w_ref, mhi_ref, mlo_ref, chi_ref, clo_ref, whi_ref, wlo_ref,
    xb_ref, fhi_ref, flo_ref, fphi_ref, fplo_ref, sq_ref, sqp_ref, sqrow_ref, spare_ref,
):
    K = 2 * HALF
    width = x_ref.shape[1]
    n_piv = p_ref.shape[0]
    blocks = n_piv // K
    fhi_ref[...], flo_ref[...] = halves(f_ref[...])
    wide = x_ref[...].astype(jnp.float32)
    sq_ref[...] = jnp.sum(wide * wide, axis=1, keepdims=True)
    ones = jnp.ones((8, width), jnp.bfloat16)
    eye = lax.broadcasted_iota(jnp.int32, (K, K), 0) == lax.broadcasted_iota(jnp.int32, (K, K), 1)

    def residual(rows, sq, f, points, sq_row, fp):
        inner = lax.dot_general(rows, points, NT, preferred_element_type=jnp.float32)
        return jnp.exp(2.0 * inner - sq - sq_row) - dot_split(f, fp, NT)

    def factor_half(start):
        rows = [w_ref[pl.ds(start + 8 * i, 8), start : start + HALF] for i in range(HALF // 8)]
        for i, row in enumerate(inverse_factor(rows, spare_ref)):
            w_ref[pl.ds(start + 8 * i, 8), start : start + HALF] = row

    def block(b, total):
        at = span(b * K, K, K)
        points = p_ref[at, :]
        xb_ref[at, :] = points.astype(jnp.bfloat16)
        fphi_ref[at, :], fplo_ref[at, :] = halves(fp_ref[at, :])
        squares = points * points
        sqp_ref[...] = jnp.sum(squares, axis=1, keepdims=True)
        sq_hi, sq_lo = halves(squares)
        sq_row = lax.dot_general(ones, sq_hi, NT, preferred_element_type=jnp.float32)
        sq_row = sq_row + lax.dot_general(ones, sq_lo, NT, preferred_element_type=jnp.float32)
        sqrow_ref[span(8 * b, 8), :] = sq_row
        sq_row = sq_row[0:1, :]
        fp = (fphi_ref[at, :], fplo_ref[at, :])
        gram_ref[...] = residual(xb_ref[at, :], sqp_ref[...], fp, xb_ref[at, :], sq_row, fp)

        def earlier(c, _):
            to = span(c * K, K, K)
            part_ref[...] = residual(
                xb_ref[at, :], sqp_ref[...], (fphi_ref[at, :], fplo_ref[at, :]),
                xb_ref[to, :], sqrow_ref[span(8 * c, 8), :][0:1, :], (fphi_ref[to, :], fplo_ref[to, :]),
            )

            def before(e, _):
                by = span(e * K, K, K)
                part_ref[...] = part_ref[...] - dot_split(
                    (mhi_ref[at, by], mlo_ref[at, by]), (mhi_ref[to, by], mlo_ref[to, by]), NT
                )
                return 0

            lax.fori_loop(0, c, before, 0)
            m = halves(dot_split(halves(part_ref[...]), (whi_ref[to, :], wlo_ref[to, :]), NT))
            mhi_ref[at, to], mlo_ref[at, to] = m
            gram_ref[...] = gram_ref[...] - dot_split(m, m, NT)
            return 0

        lax.fori_loop(0, b, earlier, 0)
        gram = gram_ref[...]
        diag = jnp.sum(jnp.where(eye, gram, 0.0), axis=0, keepdims=True)
        off = jnp.sum(jnp.abs(gram), axis=0, keepdims=True) - jnp.abs(diag)
        shift = ridge_base + jnp.maximum(jnp.max(off - diag, axis=1, keepdims=True), 0.0)
        w_ref[...] = gram + jnp.where(eye, shift, 0.0)

        c_ref[0:256, at] = residual(
            x_ref[0:256, :], sq_ref[0:256, :], (fhi_ref[0:256, :], flo_ref[0:256, :]), xb_ref[at, :], sq_row,
            (fphi_ref[at, :], fplo_ref[at, :]),
        )
        factor_half(0)
        first = w_ref[:HALF, :HALF]
        low = dot_exact(w_ref[HALF:, :HALF], first, NT)
        w_ref[HALF:, HALF:] = w_ref[HALF:, HALF:] - dot_exact(low, low, NT)
        carried = dot_exact(low, first, NN)
        c_ref[256:512, at] = residual(
            x_ref[256:512, :], sq_ref[256:512, :], (fhi_ref[256:512, :], flo_ref[256:512, :]), xb_ref[at, :], sq_row,
            (fphi_ref[at, :], fplo_ref[at, :]),
        )
        factor_half(HALF)
        w_ref[HALF:, :HALF] = -dot_exact(w_ref[HALF:, HALF:], carried, NN)
        w_ref[:HALF, HALF:] = jnp.zeros((HALF, HALF), jnp.float32)
        inverse = halves(w_ref[...])
        whi_ref[at, :], wlo_ref[at, :] = inverse


        def carry(e, _):
            by = span(e * K, K, K)
            c_ref[:, at] = c_ref[:, at] - dot_split(
                (chi_ref[:, by], clo_ref[:, by]), (mhi_ref[at, by], mlo_ref[at, by]), NT
            )
            return 0

        lax.fori_loop(0, b, carry, 0)
        cols = dot_split(halves(c_ref[:, at]), (whi_ref[at, :], wlo_ref[at, :]), NT)
        c_ref[:, at] = cols
        chi_ref[:, at], clo_ref[:, at] = halves(cols)
        squared = cols * cols
        return total + squared[:, :HALF] + squared[:, HALF:]

    total = lax.fori_loop(0, blocks, block, jnp.zeros((x_ref.shape[0], HALF), jnp.float32))
    sums = dot_exact(jnp.ones((8, HALF), jnp.float32), total, NT)
    nd_ref[...] = d_ref[...] - sums[0:1, :]


def window(x, f, diag, points, factor_rows):
    rows, width = x.shape
    rank = f.shape[1]
    n_piv = points.shape[0]
    K = 2 * HALF
    half, single = jnp.bfloat16, jnp.float32
    cols, new_diag = pl.pallas_call(
        window_kernel,
        out_shape=(
            jax.ShapeDtypeStruct((rows, n_piv), single),
            jax.ShapeDtypeStruct((1, rows), single),
        ),
        in_specs=[pl.BlockSpec(memory_space=pltpu.VMEM)] * 5,
        out_specs=[pl.BlockSpec(memory_space=pltpu.VMEM)] * 2,
        scratch_shapes=[
            pltpu.VMEM((K, K), single),
            pltpu.VMEM((K, K), single),
            pltpu.VMEM((K, K), single),
            pltpu.VMEM((n_piv, n_piv), half),
            pltpu.VMEM((n_piv, n_piv), half),
            pltpu.VMEM((rows, n_piv), half),
            pltpu.VMEM((rows, n_piv), half),
            pltpu.VMEM((n_piv, K), half),
            pltpu.VMEM((n_piv, K), half),
            pltpu.VMEM((n_piv, width), half),
            pltpu.VMEM((rows, rank), half),
            pltpu.VMEM((rows, rank), half),
            pltpu.VMEM((n_piv, rank), half),
            pltpu.VMEM((n_piv, rank), half),
            pltpu.VMEM((rows, 1), single),
            pltpu.VMEM((K, 1), single),
            pltpu.VMEM((8 * (n_piv // K), K), single),
            pltpu.VMEM((144, HALF), single),
        ],
        compiler_params=pltpu.CompilerParams(vmem_limit_bytes=30 << 20),
        name="window",
    )(x, f, diag.reshape(1, rows), points, factor_rows)
    return cols, new_diag.reshape(rows)


MESH = pl.DeviceIdType.MESH
X, Y, Z = 4, 4, 8
PICK = 256


COPIES = 4 + 6 + 6 + 7 + 7 + 6 + 6 + 5


def gather_kernel(*refs):
    n_lanes = 2
    row_ref, x_ref, f_ref = refs[:3]
    third_ref, send, recv = refs[-3:]
    refs = refs[3:-3]
    outs, picked, scratch = refs[:n_lanes], refs[n_lanes : 2 * n_lanes], refs[2 * n_lanes :]
    where = lax.axis_index("rows")
    x = lax.axis_index("sub")
    core = where % 2
    y = (where // 2) % Y
    z = where // (2 * Y)
    p1 = x * (1 - core) + y * core
    p2 = y * (1 - core) + x * core

    def device(q1, q2, qz):
        qx = q1 * (1 - core) + q2 * core
        qy = q2 * (1 - core) + q1 * core
        return ((qz * Y + qy) * 2 + core, qx)

    sibling = ((z * Y + y) * 2 + 1 - core, x)
    right1, left1 = device((p1 + 1) % X, p2, z), device((p1 + 3) % X, p2, z)
    right2, left2 = device(p1, (p2 + 1) % Y, z), device(p1, (p2 + 3) % Y, z)
    along_z = [device(p1, p2, (z + d) % Z) for d in range(1, Z)]

    barrier = pltpu.get_barrier_semaphore()
    partners = [sibling, right1, left1, right2, left2] + along_z
    for partner in partners:
        pl.semaphore_signal(barrier, inc=1, device_id=partner, device_id_type=MESH)

    rest = f_ref[...]
    for k in range(3):
        third_ref[k] = rest.astype(jnp.bfloat16)
        rest = rest - third_ref[k].astype(jnp.float32)
    local_rows = x_ref.shape[0]

    def pick(b, _):
        at = pl.ds(pl.multiple_of(b * PICK, PICK), PICK)
        places = lax.broadcasted_iota(jnp.int32, (PICK, local_rows), 1)
        chosen = jnp.where(row_ref[at, :] == places, 1.0, 0.0).astype(jnp.bfloat16)
        dot = functools.partial(jnp.dot, chosen, preferred_element_type=jnp.float32)
        picked[0][at, :] = dot(x_ref[...])
        picked[1][at, :] = (dot(third_ref[0]) + dot(third_ref[1])) + dot(third_ref[2])
        return 0

    lax.fori_loop(0, row_ref.shape[0] // PICK, pick, 0)
    pl.semaphore_wait(barrier, len(partners))

    started = []

    def copy(src, dst, target):
        k = len(started)
        made = pltpu.make_async_remote_copy(
            src_ref=src, dst_ref=dst, send_sem=send.at[k], recv_sem=recv.at[k],
            device_id=target, device_id_type=MESH,
        )
        made.start()
        started.append(made)
        return made

    def span(start, size):
        return pl.ds(pl.multiple_of(start, 8), size)

    def travel(s_ref, out_ref, sib, near1, near2, near3):
        n_piv, width = s_ref.shape
        half = n_piv // 2
        piece1, piece2, piece3 = half // X, half // X // Y, 8
        cut = width // 2

        order = (2, 1, 3, 0)
        from_sibling = {}
        for d in order:
            q = (p2 + d) % X
            from_sibling[d] = copy(
                s_ref.at[span((1 - core) * half + q * piece1, piece1), :],
                sib.at[span(q * piece1, piece1), :],
                sibling,
            )
        yield

        def merge(d):
            q = (p1 + d) % X
            from_sibling[d].wait_recv()
            at = span(q * piece1, piece1)
            sib[at, :] = sib[at, :] + s_ref[span(core * half + q * piece1, piece1), :]

        def scatter(base, piece, p, right, left, near, ready):
            hp = piece // 2

            def rows(d, part):
                return span(base + ((p + d) % 4) * piece + part * hp, hp)

            ready(2)
            over_right = copy(sib.at[rows(2, 0), :], near.at[0], right)
            over_left = copy(sib.at[rows(2, 1), :], near.at[1], left)
            ready(1)
            plain_right = copy(sib.at[rows(1, 1), :], near.at[2], right)
            ready(3)
            plain_left = copy(sib.at[rows(3, 0), :], near.at[3], left)
            ready(0)
            yield
            over_right.wait_recv()
            sib[rows(1, 0), :] = sib[rows(1, 0), :] + near[0]
            last_right = copy(sib.at[rows(1, 0), :], near.at[4], right)
            over_left.wait_recv()
            sib[rows(3, 1), :] = sib[rows(3, 1), :] + near[1]
            last_left = copy(sib.at[rows(3, 1), :], near.at[5], left)
            yield
            plain_right.wait_recv()
            sib[rows(0, 1), :] = sib[rows(0, 1), :] + near[2]
            plain_left.wait_recv()
            sib[rows(0, 0), :] = sib[rows(0, 0), :] + near[3]
            last_right.wait_recv()
            sib[rows(0, 0), :] = sib[rows(0, 0), :] + near[4]
            last_left.wait_recv()
            sib[rows(0, 1), :] = sib[rows(0, 1), :] + near[5]

        yield from scatter(0, piece1, p1, right1, left1, near1, merge)
        base2 = p1 * piece1
        yield from scatter(base2, piece2, p2, right2, left2, near2, lambda d: None)
        base3 = base2 + p2 * piece2

        def cell(base, q):
            return span(base + (q // 2) * piece3, piece3), pl.ds(
                pl.multiple_of((q % 2) * cut, 128), cut
            )

        arriving = []
        for d in range(1, Z):
            arriving.append(
                copy(sib.at[cell(base3, (z + d) % Z)], near3.at[d - 1], along_z[d - 1])
            )
        yield
        total = sib[cell(base3, z)]
        for d in range(1, Z):
            arriving[d - 1].wait_recv()
            total = total + near3[d - 1]
        mine = cell(core * half + base3, z)
        out_ref[mine] = total
        arriving = [
            copy(out_ref.at[mine], out_ref.at[mine], along_z[d - 1]) for d in range(1, Z)
        ]
        yield
        for made in arriving:
            made.wait_recv()

        def gather(base, piece, p, right, left, done):
            hp = piece // 2

            def rows(d, part, size):
                return span(base + ((p + d) % 4) * piece + part * hp, size)

            parts = [out_ref.at[rows(0, k, hp), :] for k in range(2)]
            from_left = [copy(parts[0], parts[0], right)]
            from_right = [copy(parts[1], parts[1], left)]
            from_left += [copy(parts[1], parts[1], right)]
            from_right += [copy(parts[0], parts[0], left)]
            done(rows(0, 0, piece))
            yield
            from_left[0].wait_recv()
            on = out_ref.at[rows(3, 0, hp), :]
            far_left = copy(on, on, right)
            from_right[0].wait_recv()
            on = out_ref.at[rows(1, 1, hp), :]
            far_right = copy(on, on, left)
            from_left[1].wait_recv()
            done(rows(3, 0, piece))
            from_right[1].wait_recv()
            done(rows(1, 0, piece))
            yield
            far_left.wait_recv()
            done(rows(2, 0, hp))
            far_right.wait_recv()
            done(rows(2, 1, hp))

        yield from gather(core * half + base2, piece2, p2, right2, left2, lambda at: None)
        across = []

        def hand_over(at):
            across.append(copy(out_ref.at[at, :], out_ref.at[at, :], sibling))

        yield from gather(core * half, piece1, p1, right1, left1, hand_over)
        yield
        for made in across:
            made.wait_recv()

    ways = [
        travel(picked[i], outs[i], *scratch[4 * i : 4 * i + 4]) for i in range(n_lanes)
    ]
    while ways:
        ways = [way for way in ways if next(way, True) is None]
    for made in started:
        made.wait_send()


def gather_rows(row, x, f):
    n_piv = row.shape[0]
    half = n_piv // 2
    widths = (x.shape[1], f.shape[1])
    scratch = [pltpu.VMEM((n_piv, width), jnp.float32) for width in widths]
    for width in widths:
        scratch += [
            pltpu.VMEM((half, width), jnp.float32),
            pltpu.VMEM((6, half // X // 2, width), jnp.float32),
            pltpu.VMEM((6, half // X // Y // 2, width), jnp.float32),
            pltpu.VMEM((Z - 1, 8, width // 2), jnp.float32),
        ]
    scratch += [pltpu.VMEM((3,) + f.shape, jnp.bfloat16)]
    copies = COPIES * len(widths)
    return pl.pallas_call(
        gather_kernel,
        out_shape=tuple(jax.ShapeDtypeStruct((n_piv, width), jnp.float32) for width in widths),
        in_specs=[pl.BlockSpec(memory_space=pltpu.VMEM)] * 3,
        out_specs=[pl.BlockSpec(memory_space=pltpu.VMEM)] * 2,
        scratch_shapes=scratch
        + [pltpu.SemaphoreType.DMA((copies,)), pltpu.SemaphoreType.DMA((copies,))],
        compiler_params=pltpu.CompilerParams(
            collective_id=0, has_side_effects=True, vmem_limit_bytes=40 << 20
        ),
        name="gather_rows",
    )(row, x, f)


def on_device(embeddings, factor, diagonal, pivot_owner, pivot_local):
    device = lax.axis_index("rows") * lax.axis_size("sub") + lax.axis_index("sub")
    row = jnp.where(pivot_owner == device, pivot_local, -1).reshape(-1, 1)
    points, factor_rows = gather_rows(row, embeddings, factor)
    return window(embeddings, factor, diagonal, points, factor_rows)


def solution(mesh):
    return jax.shard_map(
        on_device,
        mesh=mesh,
        in_specs=(P(("rows", "sub"), None), P(("rows", "sub"), None), P(("rows", "sub")), P(), P()),
        out_specs=(P(("rows", "sub"), None), P(("rows", "sub"))),
        check_vma=False,
    )
```
